128 devices in a mesh: ctx: 16 (over z, x), head: 4 (over y_lo, core), dp: 2 (over y_hi).
Axes of the slice: x: 4, y: 4 (y_hi: 2, y_lo: 2; y = y_hi * 2 + y_lo), z: 4, core: 2. Of those that a mesh axis runs over, the one named last changes fastest.
Arguments:
- queries: bfloat16 [2, 4096, 1536], P('dp', 'ctx', 'head'), may hold values from -12 to 12
- keys: bfloat16 [2, 4096, 1536], P('dp', 'ctx', 'head'), may hold values from -6 to 6
- values: bfloat16 [2, 4096, 1536], P('dp', 'ctx', 'head'), may hold values from -6 to 6
- grad_out: bfloat16 [2, 4096, 1536], P('dp', 'ctx', 'head'), may hold values from -6 to 6
- kv_list: int32 [64, 32], P('ctx'), may hold values from 0 to 63, as said below
- cover_lists: int32 [64, 2], P('ctx'), may hold values from 0 to 15, all different within a row
- cond_tokens: bfloat16 [2, 1024, 3072], P('dp', 'ctx'), may hold values from -6 to 6
- cond_weight: bfloat16 [3072, 1536], P(None, 'head'), may hold values from -0.109375 to 0.109375
Outputs:
- grad_query: bfloat16 [2, 4096, 1536], P('dp', 'ctx', 'head')
- grad_key: bfloat16 [2, 4096, 1536], P('dp', 'ctx', 'head')
- grad_value: bfloat16 [2, 4096, 1536], P('dp', 'ctx', 'head')
- grad_cond_weight: float32 [3072, 1536], P(('ctx', 'dp'), 'head')
The draws below stay inside these ranges and needn't reach their ends.
Inputs may be any that keep to these rules, and one draw needn't show every extreme that they name: `kv_list`: entries j * 2 to j * 2 + 1 of a row are 2 different blocks among blocks j * 4 to j * 4 + 3. `cover_lists`: the 2 entries of a row are different.
All inputs are finite; a program needn't handle non-finite values.
Results may differ from the reference program's by a relative error of at most 0.025.
Values may be sent and summed in bfloat16 or wider, within the bound.
No kernel may reach another device: no remote copies, remote signals or barrier semaphores. Data moves between devices by JAX's collectives and lax.ppermute only.
A program may use at most 128 MiB of HBM per device.

```python
import math
import jax
import jax.numpy as jnp
from jax import lax

D = 3072
HEADS = 12
HD = 128
BLK = 64
PER = 2
OV = 2
KB_DEV = 4
LENGTH = 4096
QBLOCKS = 64
KSEL = 32
LR = 1024
BATCH = 2
N_CTX = 16


def draw_queries(key, part):
    key = jax.random.fold_in(key, 1)
    full_shape = (BATCH, LENGTH, HEADS * HD)
    drawn = jnp.clip(jax.random.normal(key, full_shape, jnp.float32), -6.0, 6.0)
    return drawn.astype(jnp.bfloat16)


def draw_keys(key, part):
    key = jax.random.fold_in(key, 2)
    full_shape = (BATCH, LENGTH, HEADS * HD)
    drawn = jnp.clip(jax.random.normal(key, full_shape, jnp.float32), -6.0, 6.0)
    return drawn.astype(jnp.bfloat16)


def draw_kv_list(key, part):
    key = jax.random.fold_in(key, 3)
    ranks = jax.random.randint(key, (QBLOCKS, N_CTX, KB_DEV), 0, 1 << 20) * KB_DEV + jnp.arange(KB_DEV, dtype=jnp.int32)
    picked = jnp.argsort(ranks, axis=-1)[:, :, :PER].astype(jnp.int32)
    offsets = (jnp.arange(N_CTX, dtype=jnp.int32) * KB_DEV)[None, :, None]
    return (picked + offsets).reshape(QBLOCKS, N_CTX * PER).astype(jnp.int32)


def with_spikes(entries, rng, source, target, parts, factor):
    owner, partner = [(jnp.arange(entries.shape[dim]) // (entries.shape[dim] // parts)).reshape([-1 if axis == dim else 1 for axis in range(entries.ndim)]) for dim in (source, target)]
    chosen = jax.random.permutation(rng, parts)[partner]
    strong = (owner == chosen) | (owner == (partner + parts // 2) % parts)
    return jnp.where(strong, factor * entries, entries)


def block_scale(key, dims, cuts, smallest, top_value):
    def one(dim, shards_of):
        steps = jax.random.uniform(jax.random.fold_in(jax.random.fold_in(key, 6), dim), (shards_of,), jnp.float32, smallest / len(cuts), top_value / len(cuts))
        return jnp.repeat(jnp.exp(steps), dims[dim] // shards_of).reshape((-1,) + (1,) * (len(dims) - dim - 1))

    factor_of = one(*cuts[0])
    for cut in cuts[1:]:
        factor_of = factor_of * one(*cut)
    return factor_of


def choose_distinct(stream_key, rows, number_of, top, lift):
    order = jax.random.permutation(jax.random.fold_in(stream_key, 1), number_of)
    favour = order
    for power in range(3):
        favour = favour * favour // number_of
    favour = favour * lift // number_of
    tickets = jax.random.randint(jax.random.fold_in(stream_key, 2), (rows, number_of), 0, 4096) + favour
    fixed_rows = jax.random.permutation(jax.random.fold_in(stream_key, 3), rows)[jnp.arange(number_of) % rows]
    tickets = jnp.where(jnp.arange(rows)[:, None] == fixed_rows[None, :], 1 << 14, tickets)
    score = tickets * number_of + jnp.arange(number_of)
    return lax.top_k(score.astype(jnp.int32), top)[1].astype(jnp.int32)


def bell_draw(stream_key, shape, width, reach, pieces=(), held_as=jnp.bfloat16):
    result = jax.random.normal(stream_key, shape, jnp.float32) * width
    if len(pieces) > 0:
        result = block_scale(stream_key, shape, pieces, -0.22, 0.18) * result
    return jnp.clip(result, min=-reach, max=reach).astype(held_as)


def noise_with(key, extent, width, limit, cuts, heavy, held_as=jnp.bfloat16):
    result = width * jax.random.normal(key, extent, jnp.float32)
    if cuts:
        result = result * block_scale(key, extent, cuts, -0.22, 0.18)
    return jnp.clip(with_spikes(result, jax.random.fold_in(key, 3), *heavy), -limit, limit).astype(held_as)


def setup_inputs(seed: int = 0) -> dict:
    streams_of = jax.random.split(jax.random.key(seed), 9)
    return {
        "queries": draw_queries(jax.random.fold_in(streams_of[8], 71), 0),
        "keys": draw_keys(jax.random.fold_in(streams_of[8], 71), 0),
        "values": bell_draw(streams_of[2], (BATCH, LENGTH, HEADS * HD), 1.0, 6.0, ((0, 2), (1, 16), (2, 4))),
        "grad_out": bell_draw(streams_of[3], (BATCH, LENGTH, HEADS * HD), 1.0, 6.0, ((0, 2), (1, 16), (2, 4))),
        "kv_list": draw_kv_list(jax.random.fold_in(streams_of[8], 71), 0),
        "cover_lists": choose_distinct(streams_of[5], QBLOCKS, N_CTX, OV, 2048),
        "cond_tokens": noise_with(streams_of[6], (BATCH, LR, D), 1.0, 6.0, ((0, 2), (1, 16)), (1, 2, 16, 2.0)),
        "cond_weight": bell_draw(streams_of[7], (D, HEADS * HD), D ** -0.5, 0.109375, ((1, 4),)),
    }


def clip_grads(queries, keys, values, grad_out, kv_list, cover_lists, cond_tokens, cond_weight):
    feature_width = HEADS * HD
    score_scale = 1.0 / math.sqrt(HD)
    cond_proj = jnp.dot(cond_tokens, cond_weight, preferred_element_type=jnp.float32).astype(jnp.bfloat16)
    cond_blocks = cond_proj.reshape(N_CTX, BLK, feature_width).astype(jnp.float32)
    lifted = jnp.zeros((QBLOCKS, BLK, feature_width), jnp.float32)
    for slot_index in range(OV):
        lifted = lifted + jnp.take(cond_blocks, cover_lists[:, slot_index], axis=0)
    query_eff = (queries.reshape(QBLOCKS, BLK, feature_width).astype(jnp.float32) + lifted).astype(jnp.bfloat16)
    query_eff = query_eff.reshape(QBLOCKS, BLK, HEADS, HD)
    grad_blocks = grad_out.reshape(QBLOCKS, BLK, HEADS, HD)
    key_blocks = keys.reshape(QBLOCKS, BLK, HEADS, HD)
    value_blocks = values.reshape(QBLOCKS, BLK, HEADS, HD)

    def one_block(loop_state, inputs):
        key_acc, value_acc = loop_state
        chosen, query_here, grad_here = inputs
        key_pick = jnp.take(key_blocks, chosen, axis=0).reshape(KSEL * BLK, HEADS, HD).astype(jnp.float32)
        value_pick = jnp.take(value_blocks, chosen, axis=0).reshape(KSEL * BLK, HEADS, HD).astype(jnp.float32)
        query_float = query_here.astype(jnp.float32)
        grad_float = grad_here.astype(jnp.float32)
        scores = jnp.einsum('bhd,khd->hbk', query_float, key_pick, precision=lax.Precision.HIGHEST) * score_scale
        grad_prob = jnp.einsum('bhd,khd->hbk', grad_float, value_pick, precision=lax.Precision.HIGHEST)
        row_top = lax.optimization_barrier(jnp.max(scores, axis=-1, keepdims=True))
        log_total = row_top + jnp.log(lax.optimization_barrier(jnp.sum(jnp.exp(scores - row_top), axis=-1, keepdims=True)))
        probs_full = jnp.exp(scores - log_total)
        row_delta = lax.optimization_barrier(jnp.sum(probs_full * grad_prob, axis=-1, keepdims=True))
        probs_half = lax.optimization_barrier(probs_full.astype(jnp.bfloat16)).astype(jnp.float32)
        grad_score = (probs_full * (grad_prob - row_delta) * score_scale).astype(jnp.bfloat16)
        grad_score = lax.optimization_barrier(grad_score).astype(jnp.float32)
        query_total = jnp.einsum('hbk,khd->bhd', grad_score, key_pick, precision=lax.Precision.HIGHEST)
        key_part = jnp.einsum('hbk,bhd->khd', grad_score, query_float, precision=lax.Precision.HIGHEST)
        value_part = jnp.einsum('hbk,bhd->khd', probs_half, grad_float, precision=lax.Precision.HIGHEST)
        key_acc = key_acc.at[chosen].add(key_part.reshape(KSEL, BLK, HEADS, HD))
        value_acc = value_acc.at[chosen].add(value_part.reshape(KSEL, BLK, HEADS, HD))
        return ((key_acc, value_acc), query_total)
    zero_acc = jnp.zeros((QBLOCKS, BLK, HEADS, HD), jnp.float32)
    (key_acc, value_acc), query_total = lax.scan(one_block, (zero_acc, zero_acc), (kv_list, query_eff, grad_blocks))
    owners = lax.optimization_barrier(jnp.sum((cover_lists[:, :, None] == jnp.arange(N_CTX, dtype=jnp.int32)[None, None, :]).astype(jnp.float32), axis=1))
    cond_grad = jnp.einsum('bo,bf->of', owners, query_total.reshape(QBLOCKS, BLK * feature_width), precision=lax.Precision.HIGHEST)
    cond_half = cond_grad.reshape(LR, feature_width).astype(jnp.bfloat16)
    weight_term = jnp.dot(cond_tokens.T, cond_half, preferred_element_type=jnp.float32)
    grad_query = query_total.reshape(LENGTH, feature_width).astype(jnp.bfloat16)
    grad_key = key_acc.reshape(LENGTH, feature_width).astype(jnp.bfloat16)
    grad_value = value_acc.reshape(LENGTH, feature_width).astype(jnp.bfloat16)
    return (grad_query, grad_key, grad_value, weight_term)

def reference(queries, keys, values, grad_out, kv_list, cover_lists, cond_tokens, cond_weight):
    query_list = []
    key_list = []
    value_list = []
    weight_sum = jnp.zeros((D, HEADS * HD), jnp.float32)
    for clip_index in range(BATCH):
        grad_query, grad_key, grad_value, weight_term = clip_grads(queries[clip_index], keys[clip_index], values[clip_index], grad_out[clip_index], kv_list, cover_lists, cond_tokens[clip_index], cond_weight)
        query_list.append(grad_query)
        key_list.append(grad_key)
        value_list.append(grad_value)
        weight_sum = weight_sum + weight_term
    return (jnp.stack(query_list), jnp.stack(key_list), jnp.stack(value_list), weight_sum)
```

```python
import math

import jax
import jax.numpy as jnp
import numpy as np
from jax import lax
from jax.experimental import pallas as pl
from jax.experimental.pallas import tpu as pltpu
from jax.sharding import PartitionSpec as P

HD = 128
BLK = 64
PER = 2
HEADS = 3
WIDTH = HEADS * HD
SIDE = 4
ROWS = 1024
SCALE = 1.0 / math.sqrt(HD)
LOG2E = 1.4426950408889634
SCALE2 = SCALE * LOG2E
OFFSETS = (0, -1, 1, 2)
SLOT_OF = {0: 0, 3: 1, 1: 2, 2: 3}
BF16 = jnp.bfloat16
F32 = jnp.float32
MIB = 1 << 20
CHUNK = 192
PADDED = 256


def roles(ctx, core):
    z, x = divmod(ctx, SIDE)
    return (x, z) if core == 0 else (z, x)


def ctx_of(u, v, core):
    return v * SIDE + u if core == 0 else u * SIDE + v


def info_table():
    table = np.zeros((2, SIDE * SIDE, 64), np.int32)
    for core in range(2):
        for ctx in range(SIDE * SIDE):
            u, v = roles(ctx, core)
            row = table[core, ctx]
            for slot, off in enumerate(OFFSETS):
                row[slot] = ctx_of(u, (v + off) % SIDE, core)
            for owner in range(SIDE * SIDE):
                uo, vo = roles(owner, core)
                place = SLOT_OF[(vo - v) % SIDE] * SIDE + SLOT_OF[(uo - u) % SIDE]
                row[4 + owner] = place
                row[20 + place] = owner
    return table


INFO = info_table()


def send(array, role, by):
    pairs = []
    for ctx in range(SIDE * SIDE):
        for head in range(4):
            core = head % 2
            u, v = roles(ctx, core)
            if role == "u":
                target = ctx_of((u + by) % SIDE, v, core)
            else:
                target = ctx_of(u, (v + by) % SIDE, core)
            pairs.append((ctx * 4 + head, target * 4 + head))
    return lax.ppermute(array, ("ctx", "head"), pairs)


def gathered(array, role):
    return [array] + [send(array, role, -off) for off in OFFSETS[1:]]


def scattered(parts, role):
    return [parts[0]] + [send(parts[slot], role, OFFSETS[slot]) for slot in range(1, SIDE)]


def summed(parts):
    total = parts[0].astype(F32)
    for part in parts[1:]:
        total = total + part.astype(F32)
    return total


def aligned(ref, off):
    parts = []
    for mine in OFFSETS:
        slot = SLOT_OF[(mine - off) % SIDE]
        parts.append(ref[:, slot * 256 : (slot + 1) * 256])
    return jnp.concatenate(parts, axis=1)


def nt(a, b):
    return lax.dot_general(a, b, (((1,), (1,)), ((), ())), preferred_element_type=F32)


def nn(a, b):
    return lax.dot_general(a, b, (((1,), (0,)), ((), ())), preferred_element_type=F32)


def tn(a, b):
    return lax.dot_general(a, b, (((0,), (0,)), ((), ())), preferred_element_type=F32)


def picks(info, lists, block):
    starts = []
    for slot in range(SIDE):
        shard = info[slot]
        for j in range(PER):
            local = lists[block, shard * PER + j] - shard * SIDE
            starts.append((slot, pl.multiple_of(local * BLK, BLK)))
    return starts


def taken(refs, starts, head):
    cols = slice(head * HD, (head + 1) * HD)
    return jnp.concatenate([refs[slot][pl.ds(at, BLK), cols] for slot, at in starts], axis=0)


def cover_places(info, lists, block):
    return [info[4 + lists[block, 32 + j]] for j in range(2)]


def score_kernel(info, lists, *refs):
    q, c, k = refs[0:4], refs[4:8], refs[8:12]
    qeff, stat, cbuf, cols = refs[12:]
    for slot in range(SIDE):
        cbuf[slot * 256 : (slot + 1) * 256, :] = c[slot][...]
        qeff[slot * 256 : (slot + 1) * 256, :] = q[slot][...]
    lane = lax.broadcasted_iota(jnp.int32, (BLK, HD), 1)

    def step(block, carry):
        rows = pl.ds(pl.multiple_of(block * BLK, BLK), BLK)
        places = cover_places(info, lists, block)
        lifted = [cbuf[pl.ds(pl.multiple_of(at * BLK, BLK), BLK), :].astype(F32) for at in places]
        query = (qeff[rows, :].astype(F32) + (lifted[0] + lifted[1])).astype(BF16)
        qeff[rows, :] = query
        starts = picks(info, lists, block)
        tile = jnp.zeros((BLK, HD), F32)
        for head in range(HEADS):
            scores = nt(query[:, head * HD : (head + 1) * HD], taken(k, starts, head))
            top = jnp.max(scores, axis=1, keepdims=True)
            total = jnp.sum(jnp.exp2((scores - top) * SCALE2), axis=1, keepdims=True)
            tile = jnp.where(lane == head, top, tile)
            tile = jnp.where(lane == HEADS + head, total, tile)
        cols[rows, :] = tile
        return carry

    lax.fori_loop(0, 16, step, 0)
    stat[...] = cols[...].T[0:8, :]


def value_kernel(info, lists, *refs):
    stats, qeff = refs[0:4], refs[4]
    k, grad, v = refs[5:9], refs[9:13], refs[13:17]
    dv, delta, lrow, grad_all = refs[17:21], refs[21], refs[22], refs[23]
    cols, dcols, wide, acc = refs[24:]
    stat = [stats[0][...]] + [aligned(stats[slot], OFFSETS[slot]) for slot in range(1, SIDE)]
    tops = [s[0:HEADS] for s in stat]
    top = jnp.maximum(jnp.maximum(tops[0], tops[1]), jnp.maximum(tops[2], tops[3]))
    total = jnp.zeros_like(top)
    for s, t in zip(stat, tops):
        total = total + s[HEADS : 2 * HEADS] * jnp.exp2((t - top) * SCALE2)
    log_total = top * SCALE2 + jnp.log(total) * LOG2E
    wide[...] = jnp.zeros_like(wide)
    wide[0:HEADS, :] = log_total
    lrow[...] = wide[0:8, :]
    cols[...] = wide[...].T
    acc[...] = jnp.zeros_like(acc)
    for slot in range(SIDE):
        grad_all[slot * 256 : (slot + 1) * 256, :] = grad[slot][...]
    lane = lax.broadcasted_iota(jnp.int32, (BLK, HD), 1)

    def step(block, carry):
        rows = pl.ds(pl.multiple_of(block * BLK, BLK), BLK)
        query, grad_here = qeff[rows, :], grad_all[rows, :]
        log_here = cols[rows, :]
        starts = picks(info, lists, block)
        tile = jnp.zeros((BLK, HD), F32)
        for head in range(HEADS):
            at = slice(head * HD, (head + 1) * HD)
            scores = nt(query[:, at], taken(k, starts, head))
            probs = jnp.exp2(scores * SCALE2 - log_here[:, head : head + 1])
            grad_prob = nt(grad_here[:, at], taken(v, starts, head))
            part = jnp.sum(probs * grad_prob, axis=1, keepdims=True)
            tile = jnp.where(lane == head, part, tile)
            value_part = tn(probs.astype(BF16), grad_here[:, at])
            for n, (slot, start) in enumerate(starts):
                acc[slot, pl.ds(start, BLK), at] += value_part[n * BLK : (n + 1) * BLK]
        dcols[rows, :] = tile
        return carry

    lax.fori_loop(0, 16, step, 0)
    delta[...] = dcols[...].T[0:8, :]
    for slot in range(SIDE):
        dv[slot][...] = acc[slot].astype(BF16)


def grad_kernel(info, lists, *refs):
    lrow, deltas, qeff, grad_all = refs[0], refs[1:5], refs[5], refs[6]
    k, v = refs[7:11], refs[11:15]
    dq, cg, dk = refs[15:19], refs[19:23], refs[23:27]
    cols, wide, qbuf, acc, cond = refs[27:]
    delta = deltas[0][...]
    for slot in range(1, SIDE):
        delta = delta + aligned(deltas[slot], OFFSETS[slot])
    wide[...] = jnp.zeros_like(wide)
    wide[0:8, :] = lrow[...]
    wide[8:16, :] = delta
    cols[...] = wide[...].T
    acc[...] = jnp.zeros_like(acc)
    cond[...] = jnp.zeros_like(cond)

    def step(block, carry):
        rows = pl.ds(pl.multiple_of(block * BLK, BLK), BLK)
        query, grad_here = qeff[rows, :], grad_all[rows, :]
        col = cols[rows, :]
        starts = picks(info, lists, block)
        parts = []
        for head in range(HEADS):
            at = slice(head * HD, (head + 1) * HD)
            keys = taken(k, starts, head)
            scores = nt(query[:, at], keys)
            probs = jnp.exp2(scores * SCALE2 - col[:, head : head + 1])
            grad_prob = nt(grad_here[:, at], taken(v, starts, head))
            grad_score = (probs * (grad_prob - col[:, 8 + head : 9 + head]) * SCALE).astype(BF16)
            parts.append(nn(grad_score, keys))
            key_part = tn(grad_score, query[:, at])
            for n, (slot, start) in enumerate(starts):
                acc[slot, pl.ds(start, BLK), at] += key_part[n * BLK : (n + 1) * BLK]
        query_part = jnp.concatenate(parts, axis=1)
        qbuf[rows, :] = query_part.astype(BF16)
        for place in cover_places(info, lists, block):
            turned = (place & 3) * 4 + (place >> 2)
            cond[pl.ds(pl.multiple_of(turned * BLK, BLK), BLK), :] += query_part
        return carry

    lax.fori_loop(0, 16, step, 0)
    for slot in range(SIDE):
        dq[slot][...] = qbuf[slot * 256 : (slot + 1) * 256, :]
        cg[slot][...] = cond[slot * 256 : (slot + 1) * 256, :].astype(BF16)
        dk[slot][...] = acc[slot].astype(BF16)


def token_kernel(info, tokens, *refs):
    out, padded = refs[0:4], refs[4]
    padded[...] = jnp.zeros_like(padded)
    for n in range(16):
        padded[:, n * PADDED : n * PADDED + CHUNK] = tokens[:, n * CHUNK : (n + 1) * CHUNK]
    for sv in range(SIDE):
        for su in range(SIDE):
            start = pl.multiple_of(info[20 + sv * SIDE + su] * PADDED, PADDED)
            out[sv][:, su * PADDED : (su + 1) * PADDED] = padded[:, pl.ds(start, PADDED)]


def weight_kernel(*refs):
    cond, tokens, out = refs[0:4], refs[4:8], refs[8:12]
    total = cond[0][...].astype(F32)
    for slot in range(1, SIDE):
        parts = []
        for mine in OFFSETS:
            at = SLOT_OF[(mine - OFFSETS[slot]) % SIDE]
            parts.append(cond[slot][at * BLK : (at + 1) * BLK, :])
        total = total + jnp.concatenate(parts, axis=0).astype(F32)
    half = total.astype(BF16)
    stacked = jnp.concatenate([t[...] for t in tokens], axis=0)
    for su in range(SIDE):
        part = tn(stacked[:, su * PADDED : (su + 1) * PADDED], half)
        out[su][...] = part[0:CHUNK, :].astype(BF16)


VMEM = pl.BlockSpec(memory_space=pltpu.VMEM)
SMEM = pl.BlockSpec(memory_space=pltpu.SMEM)


def call(kernel, name, scalars, arrays, outs, scratch, limit, flops=0, moved=0, exps=0):
    return pl.pallas_call(
        kernel,
        name=name,
        out_shape=[jax.ShapeDtypeStruct(shape, dtype) for shape, dtype in outs],
        in_specs=[SMEM] * len(scalars) + [VMEM] * len(arrays),
        out_specs=[VMEM] * len(outs),
        scratch_shapes=[pltpu.VMEM(shape, dtype) for shape, dtype in scratch],
        compiler_params=pltpu.CompilerParams(vmem_limit_bytes=limit * MIB),
        cost_estimate=pl.CostEstimate(flops=flops, bytes_accessed=moved, transcendentals=exps),
    )(*scalars, *arrays)


PRODUCT = 2 * 201326592
EXPS = 1572864


def body(queries, keys, values, grad_out, kv_list, cover_lists, cond_tokens, cond_weight):
    ctx = lax.axis_index("ctx")
    core = lax.axis_index("head") % 2
    info = lax.dynamic_slice(jnp.asarray(INFO), (core, ctx, 0), (1, 1, 64)).reshape(64)
    shard = ((256, WIDTH), BF16)
    q = gathered(queries[0], "u")
    k = gathered(keys[0], "v")
    cond_proj = jnp.dot(cond_tokens[0], cond_weight, preferred_element_type=F32).astype(BF16)
    lists_here = jnp.concatenate([kv_list, cover_lists], axis=1).astype(BF16)
    lists_here = jnp.pad(lists_here, ((0, 12), (0, WIDTH - 34)))
    row = gathered(jnp.concatenate([cond_proj, lists_here], axis=0), "u")
    lists = jnp.concatenate([part[BLK : BLK + 4, :HD] for part in row]).astype(jnp.int32)
    cond_all = gathered(jnp.concatenate([part[:BLK] for part in row]), "v")
    grad = gathered(grad_out[0], "u")
    v = gathered(values[0], "v")
    qeff, stat = call(
        score_kernel,
        "scores",
        [info, lists],
        q + cond_all + k,
        [((ROWS, WIDTH), BF16), ((8, ROWS), F32)],
        [((ROWS, WIDTH), BF16), ((ROWS, HD), F32)],
        16,
        PRODUCT,
        4 * MIB,
        EXPS,
    )
    stats = gathered(stat, "u")
    out = call(
        value_kernel,
        "values",
        [info, lists],
        stats + [qeff] + k + grad + v,
        [shard] * 4 + [((8, ROWS), F32)] * 2 + [((ROWS, WIDTH), BF16)],
        [((ROWS, HD), F32)] * 2 + [((HD, ROWS), F32), ((SIDE, 256, WIDTH), F32)],
        24,
        3 * PRODUCT,
        6 * MIB,
        EXPS,
    )
    dv, delta, lrow, grad_all = out[0:4], out[4], out[5], out[6]
    deltas = gathered(delta, "u")
    dv = scattered(dv, "v")
    tokens = call(
        token_kernel,
        "tokens",
        [info],
        [cond_tokens[0]],
        [((BLK, 4 * PADDED), BF16)] * 4,
        [((BLK, 16 * PADDED), BF16)],
        8,
        0,
        MIB,
    )
    tokens = scattered(tokens, "v")
    tokens = [tokens[0], tokens[2], tokens[1], tokens[3]]
    out = call(
        grad_kernel,
        "grads",
        [info, lists],
        [lrow] + deltas + [qeff, grad_all] + k + v,
        [shard] * 12,
        [
            ((ROWS, HD), F32),
            ((HD, ROWS), F32),
            ((ROWS, WIDTH), BF16),
            ((SIDE, 256, WIDTH), F32),
            ((ROWS, WIDTH), F32),
        ],
        24,
        4 * PRODUCT,
        7 * MIB,
        EXPS,
    )
    cond_part = summed(scattered(out[4:8], "u")).astype(BF16)
    dq = scattered(out[0:4], "u")
    dk = scattered(out[8:12], "v")
    cond_parts = gathered(cond_part, "v")
    weight = call(
        weight_kernel,
        "weights",
        [],
        cond_parts + tokens,
        [((CHUNK, WIDTH), BF16)] * 4,
        [],
        8,
        2 * 100663296,
        MIB,
    )
    weight = summed(scattered(weight, "u"))
    dp = lax.axis_index("dp")
    mine = lax.dynamic_slice_in_dim(weight, dp * 96, 96, 0)
    other = lax.dynamic_slice_in_dim(weight, (1 - dp) * 96, 96, 0).astype(BF16)
    grad_cond_weight = mine + lax.ppermute(other, "dp", [(0, 1), (1, 0)]).astype(F32)
    grad_query = summed(dq).astype(BF16)[None]
    grad_key = summed(dk).astype(BF16)[None]
    grad_value = summed(dv).astype(BF16)[None]
    return (grad_query, grad_key, grad_value, grad_cond_weight)


def solution(mesh):
    return jax.shard_map(
        body,
        mesh=mesh,
        in_specs=(
            P("dp", "ctx", "head"),
            P("dp", "ctx", "head"),
            P("dp", "ctx", "head"),
            P("dp", "ctx", "head"),
            P("ctx", None),
            P("ctx", None),
            P("dp", "ctx", None),
            P(None, "head"),
        ),
        out_specs=(
            P("dp", "ctx", "head"),
            P("dp", "ctx", "head"),
            P("dp", "ctx", "head"),
            P(("ctx", "dp"), "head"),
        ),
        check_vma=False,
    )
```

```python
import math

import jax
import jax.numpy as jnp
import numpy as np
from jax import lax
from jax.experimental import pallas as pl
from jax.experimental.pallas import tpu as pltpu
from jax.sharding import PartitionSpec as P

HD = 128
BLK = 64
PER = 2
HEADS = 3
WIDTH = HEADS * HD
SIDE = 4
ROWS = 1024
SCALE = 1.0 / math.sqrt(HD)
LOG2E = 1.4426950408889634
SCALE2 = SCALE * LOG2E
MASKS = (0, 1, 3, 2)
SLOT_OF = {0: 0, 1: 1, 3: 2, 2: 3}
BF16 = jnp.bfloat16
F32 = jnp.float32
MIB = 1 << 20
CHUNK = 192
PADDED = 256
PAIRS = 2


def roles(ctx, core):
    z, x = divmod(ctx, SIDE)
    return (x, z) if core == 0 else (z, x)


def ctx_of(u, v, core):
    return v * SIDE + u if core == 0 else u * SIDE + v


def info_table():
    table = np.zeros((2, SIDE * SIDE, 64), np.int32)
    for core in range(2):
        for ctx in range(SIDE * SIDE):
            u, v = roles(ctx, core)
            row = table[core, ctx]
            for slot, mask in enumerate(MASKS):
                row[slot] = ctx_of(u, v ^ mask, core)
                row[52 + slot] = v ^ mask
            for owner in range(SIDE * SIDE):
                uo, vo = roles(owner, core)
                place = SLOT_OF[vo ^ v] * SIDE + SLOT_OF[uo ^ u]
                row[4 + owner] = place
                row[20 + place] = owner
                row[36 + owner] = SLOT_OF[uo ^ u] * SIDE + vo
    return table


INFO = info_table()


def send(array, role, mask, clip=0):
    pairs = []
    for ctx in range(SIDE * SIDE):
        for head in range(4):
            core = head % 2
            u, v = roles(ctx, core)
            target = ctx_of(u ^ mask, v, core) if role == "u" else ctx_of(u, v ^ mask, core)
            for dp in range(2):
                source = (ctx * 4 + head) * 2 + dp
                pairs.append((source, (target * 4 + head) * 2 + (dp ^ clip)))
    return lax.ppermute(array, ("ctx", "head", "dp"), pairs)


def gathered(array, role):
    return [array] + [send(array, role, mask) for mask in MASKS[1:]]


def scattered(parts, role):
    return parts[:1] + [send(parts[slot], role, MASKS[slot]) for slot in range(1, SIDE)]


def halved(near, away, role, first, second):
    half = near.shape[0] // 2
    come = send(away, role, first)

    on = (near[half:].astype(F32) + come[half:].astype(F32)).astype(BF16)
    return [near[:half], come[:half], send(on, role, second)], on


def summed(parts):
    total = parts[0].astype(F32)
    for part in parts[1:]:
        total = total + part.astype(F32)
    return total


def aligned(ref, mask):
    parts = []
    for mine in MASKS:
        slot = SLOT_OF[mine ^ mask]
        parts.append(ref[:, slot * 256 : (slot + 1) * 256])
    return jnp.concatenate(parts, axis=1)


def nt(a, b):
    return lax.dot_general(a, b, (((1,), (1,)), ((), ())), preferred_element_type=F32)


def nn(a, b):
    return lax.dot_general(a, b, (((1,), (0,)), ((), ())), preferred_element_type=F32)


def tn(a, b):
    return lax.dot_general(a, b, (((0,), (0,)), ((), ())), preferred_element_type=F32)


def picks(info, lists, pair, slot):
    shard = info[slot]
    starts = []
    for block in range(2):
        row = (pair // 2) * 8 + (pair % 2) * 2 + block
        local = [lists[row, shard * PER + j] - shard * SIDE for j in range(PER)]
        starts.append([pl.multiple_of(at * BLK, BLK) for at in local])
    return starts


def columns(head):
    return slice(head * HD, (head + 1) * HD)


def taken(source, starts, head):
    ref, first = source
    at = columns(head)
    rows = [
        jnp.concatenate(
            [ref[pl.ds(first + starts[block][j], BLK), at] for block in range(2)], axis=1
        )
        for j in range(PER)
    ]
    return jnp.concatenate(rows, axis=0)


def diagonal(pair_rows):
    nothing = jnp.zeros((BLK, HD), pair_rows.dtype)
    return jnp.concatenate(
        [
            jnp.concatenate([pair_rows[:BLK], nothing], axis=1),
            jnp.concatenate([nothing, pair_rows[BLK:]], axis=1),
        ],
        axis=0,
    )


def all_taken(sources, starts, head):
    return jnp.concatenate(
        [taken(sources[slot], starts[slot], head) for slot in range(SIDE)], axis=0
    )


def spread(acc, starts, head, part):
    at = columns(head)
    for slot in range(SIDE):
        for j in range(PER):
            for block in range(2):
                row = slot * HD + j * BLK
                piece = part[row : row + BLK, block * HD : (block + 1) * HD]
                acc[slot][pl.ds(starts[slot][block][j], BLK), at] += piece


def covers(lists, block):
    return [lists[(block // 4) * 8 + 4 + j, block % 4] for j in range(2)]


def cover_places(info, lists, block):
    return [info[4 + owner] for owner in covers(lists, block)]


def pack_kernel(queries, grads, cond, kv_list, cover_lists, out, row, lists):
    lists[...] = jnp.zeros_like(lists)
    lists[0:4, 0:32] = kv_list[...].astype(F32)
    lists[4:6, 0:4] = cover_lists[...].astype(F32)
    row[0:BLK, :] = cond[...]
    row[BLK : BLK + 16, :] = lists[...].astype(BF16)
    out[0:256, :] = queries[...]
    out[256:512, :] = grads[...]
    out[512:592, :] = row[...]


def stack_kernel(upper, lower, _, out):
    half = upper.shape[0]
    out[0:half, :] = upper[...]
    out[half:, :] = lower[...]


def token_kernel(info, tokens, *refs):
    out, held, padded, sem = refs[0:4], refs[4], refs[5], refs[6]
    copy = pltpu.make_async_copy(tokens, held, sem)
    copy.start()
    copy.wait()
    for n in range(16):
        padded[:, n * PADDED : n * PADDED + CHUNK] = held[:, n * CHUNK : (n + 1) * CHUNK]
    for sv in range(SIDE):
        for su in range(SIDE):
            start = pl.multiple_of(info[20 + sv * SIDE + su] * PADDED, PADDED)
            columns_here = padded[:, pl.ds(start, PADDED)]
            row = (su // 2) * BLK
            at = (su % 2) * CHUNK
            out[sv][row : row + BLK, at : at + CHUNK] = columns_here[:, 0:CHUNK]


def join_kernel(*refs):
    parts, tokens, out, lists = refs[0:4], refs[4:8], refs[8:12], refs[12]
    for slot in range(SIDE):
        first = parts[slot].shape[0] - BLK - 16
        rows = parts[slot][first + BLK : first + BLK + 16, 0:HD].astype(F32)
        lists[slot * 8 : (slot + 1) * 8, :] = rows[0:8, :].astype(jnp.int32)
        for other in range(SIDE):
            out[other][slot * BLK : (slot + 1) * BLK, :] = parts[slot][first : first + BLK, :]
        out[slot][256:384, :] = tokens[slot][...]


def sum_kernel(*refs):
    total = refs[0][...].astype(F32)
    for part in refs[1:4]:
        total = total + part[...].astype(F32)
    refs[-1][...] = total.astype(refs[-1].dtype)


def split_kernel(clip, *refs):
    mine, other, total = refs[-3:]
    total[...] = refs[0][...].astype(F32)
    for part in refs[1:4]:
        total[...] += part[...].astype(F32)
    mine[...] = total[pl.ds(pl.multiple_of(clip[0] * 96, 96), 96), :]
    other[...] = total[pl.ds(pl.multiple_of(96 - clip[0] * 96, 96), 96), :].astype(BF16)


def slope_kernel(info, lists, *refs):
    qg, kv, slope_out, grad_out = refs[0:4], refs[4:8], refs[8], refs[9]
    grads = refs[10]
    step = pl.program_id(0)
    values = [(ref, 256) for ref in kv]

    @pl.when(step == 0)
    def _():
        for slot in range(SIDE):
            grads[slot * 256 : (slot + 1) * 256, :] = qg[slot][256:512, :]

    for n in range(PAIRS):
        pair = step * PAIRS + n
        rows = pl.ds(pl.multiple_of(pair * HD, HD), HD)
        grad = grads[rows, :]
        grad_out[n * HD : (n + 1) * HD, :] = grad
        starts = [picks(info, lists, pair, slot) for slot in range(SIDE)]
        for head in range(HEADS):
            slope_out[n, head] = nt(
                all_taken(values, starts, head), diagonal(grad[:, columns(head)])
            )


def score_kernel(info, lists, *refs):
    qg, kv, conds, slope = refs[0:4], refs[4:8], refs[8:12], refs[12]
    qeff, stat, probs_out, tokens = refs[13:17]
    queries, cond, sems = refs[17:]
    step = pl.program_id(0)
    copies = []
    for slot in range(SIDE):
        for half in range(2):
            source = conds[slot].at[256 + half * BLK : 256 + (half + 1) * BLK, :]
            to = tokens.at[half, slot * BLK : (slot + 1) * BLK, :]
            copies.append(pltpu.make_async_copy(source, to, sems.at[2 * slot + half]))
    keys = [(ref, 0) for ref in kv]

    @pl.when(step == 0)
    def _():
        for copy in copies:
            copy.start()
        for slot in range(SIDE):
            at = slice(slot * 256, (slot + 1) * 256)
            queries[at, :] = qg[slot][0:256, :]
            cond[at, :] = conds[slot][0:256, :]

    for n in range(PAIRS):
        pair = step * PAIRS + n
        rows = pl.ds(pl.multiple_of(pair * HD, HD), HD)
        here = slice(n * HD, (n + 1) * HD)
        lifted = []
        for block in range(2):
            places = cover_places(info, lists, 2 * pair + block)
            parts = [
                cond[pl.ds(pl.multiple_of(at * BLK, BLK), BLK), :].astype(F32) for at in places
            ]
            lifted.append(parts[0] + parts[1])
        query = (queries[rows, :].astype(F32) + jnp.concatenate(lifted, axis=0)).astype(BF16)
        qeff[here, :] = query
        starts = [picks(info, lists, pair, slot) for slot in range(SIDE)]
        tops, totals, weighted = [], [], []
        for head in range(HEADS):
            scores = nt(all_taken(keys, starts, head), diagonal(query[:, columns(head)]))
            top = jnp.max(scores, axis=0, keepdims=True)
            probs = jnp.exp2((scores - top) * SCALE2)
            tops.append(top)
            totals.append(jnp.sum(probs, axis=0, keepdims=True))
            weighted.append(jnp.sum(probs * slope[n, head], axis=0, keepdims=True))
            probs_out[n, head] = probs.astype(BF16)
        nothing = [jnp.zeros((16 - 3 * HEADS, HD), F32)]
        stat[:, here] = jnp.concatenate(tops + totals + weighted + nothing, axis=0)

    @pl.when(step == 8 // PAIRS - 1)
    def _():
        for copy in copies:
            copy.wait()


def turn_kernel(*refs):
    kv, low, high = refs[0:4], refs[5], refs[6]
    left = lax.broadcasted_iota(jnp.int32, (HD, HD), 1) < BLK

    def turn(head, carry):
        at = pl.ds(pl.multiple_of(head * HD, HD), HD)
        for slot in range(SIDE):
            for half in range(2):
                tile = kv[slot][half * HD : (half + 1) * HD, at].astype(F32).T
                rolled = pltpu.roll(tile, BLK, 1)
                block = slot * SIDE + 2 * half
                low[block, at, :] = jnp.where(left, tile, 0.0).astype(BF16)
                high[block, at, :] = jnp.where(left, 0.0, rolled).astype(BF16)
                low[block + 1, at, :] = jnp.where(left, rolled, 0.0).astype(BF16)
                high[block + 1, at, :] = jnp.where(left, 0.0, tile).astype(BF16)
        return carry

    lax.fori_loop(0, HEADS, turn, 0)


def query_kernel(info, lists, *refs):
    stats, probs_in, slope_in = refs[0:4], refs[4], refs[5]
    low, high = refs[6], refs[7]
    cg, dq, probs_out, score_out = refs[8:12], refs[12:14], refs[14], refs[15]
    factors, deltas, cond, qbuf = refs[16:]
    step = pl.program_id(0)

    @pl.when(step == 0)
    def _():
        stat = [stats[0][...]] + [aligned(stats[slot], MASKS[slot]) for slot in range(1, SIDE)]
        tops = [s[0:HEADS] for s in stat]
        top = jnp.maximum(jnp.maximum(tops[0], tops[1]), jnp.maximum(tops[2], tops[3]))
        total = jnp.zeros_like(top)
        weighted = jnp.zeros_like(top)
        for s, t in zip(stat, tops):
            share = jnp.exp2((t - top) * SCALE2)
            total = total + s[HEADS : 2 * HEADS] * share
            weighted = weighted + s[2 * HEADS : 3 * HEADS] * share
        factors[0:HEADS, :] = jnp.exp2((tops[0] - top) * SCALE2) / total
        deltas[0:HEADS, :] = weighted / total
        cond[...] = jnp.zeros_like(cond)

    left = lax.broadcasted_iota(jnp.int32, (HD, HD), 1) < BLK
    for n in range(PAIRS):
        pair = step * PAIRS + n
        rows = pl.ds(pl.multiple_of(pair * HD, HD), HD)
        starts = [picks(info, lists, pair, slot) for slot in range(SIDE)]
        parts = []
        for head in range(HEADS):
            at = columns(head)
            factor, delta = factors[head : head + 1, rows], deltas[head : head + 1, rows]
            probs = probs_in[n, head].astype(F32) * factor
            score = (probs * (slope_in[n, head] - delta) * SCALE).astype(BF16)
            probs_out[n, head] = probs.astype(BF16)
            score_out[n, head] = score
            keys = []
            for block in range(2):
                across = []
                for slot in range(SIDE):
                    one = [slot * SIDE + (starts[slot][block][j] >> 6) for j in range(PER)]
                    across.append(low[one[0], at, :] + high[one[1], at, :])
                keys.append(jnp.concatenate(across, axis=1))
            turned = nn(jnp.concatenate(keys, axis=0), score)
            parts.append(jnp.where(left, turned[:HD], turned[HD:]).T)
        query_part = jnp.concatenate(parts, axis=1)
        qbuf[rows, :] = query_part.astype(BF16)
        for block in range(2):
            for owner in covers(lists, 2 * pair + block):
                to = info[36 + owner]
                cond[pl.ds(pl.multiple_of(to * BLK, BLK), BLK), :] += query_part[
                    block * BLK : (block + 1) * BLK
                ]

    @pl.when(step == 8 // PAIRS - 1)
    def _():
        for slot in range(SIDE):
            at = slice(slot * 256, (slot + 1) * 256)
            cg[slot][...] = cond[at, :].astype(BF16)
            dq[slot // 2][(slot % 2) * 256 : (slot % 2 + 1) * 256, :] = qbuf[at, :]


def key_kernel(info, lists, probs_in, score_in, qeff, grads, *refs):
    dkv, flag, dk, dv = refs[0:2], refs[2], refs[3:7], refs[7:11]
    step = pl.program_id(0)

    @pl.when(step == 0)
    def _():
        flag[...] = jnp.zeros_like(flag)
        for one in dk + dv:
            one[...] = jnp.zeros_like(one)

    for n in range(PAIRS):
        pair = step * PAIRS + n
        here = slice(n * HD, (n + 1) * HD)
        starts = [picks(info, lists, pair, slot) for slot in range(SIDE)]
        for head in range(HEADS):
            at = columns(head)
            spread(dk, starts, head, nn(score_in[n, head], diagonal(qeff[here, at])))
            spread(dv, starts, head, nn(probs_in[n, head], diagonal(grads[here, at])))

    @pl.when(step == 8 // PAIRS - 1)
    def _():
        for slot in range(SIDE):
            half = (slot // 2) * 512
            dkv[slot % 2][half : half + 256, :] = dk[slot][...].astype(BF16)
            dkv[slot % 2][half + 256 : half + 512, :] = dv[slot][...].astype(BF16)


def weight_kernel(info, *refs):
    cond, tokens, out = refs[0], refs[1], refs[2:6]
    whole, stacked, sem = refs[6:]
    copy = pltpu.make_async_copy(tokens, stacked, sem)
    copy.start()
    rows = []
    for slot in range(SIDE):
        rows.append(cond[pl.ds(pl.multiple_of(info[52 + slot] * BLK, BLK), BLK), :])
    half_sums = jnp.concatenate(rows, axis=0)
    copy.wait()
    for half in range(2):
        whole[...] = tn(stacked[half], half_sums)
        for n in range(2):
            out[2 * half + n][...] = whole[n * CHUNK : (n + 1) * CHUNK, :].astype(BF16)


VMEM = pl.BlockSpec(memory_space=pltpu.VMEM)
SMEM = pl.BlockSpec(memory_space=pltpu.SMEM)
ANY = pl.BlockSpec(memory_space=pl.ANY)
HBM = pl.BlockSpec(memory_space=pltpu.HBM)
TILES = pl.BlockSpec((PAIRS, HEADS, 512, HD), lambda i: (i, 0, 0, 0))
LINES = pl.BlockSpec((PAIRS * HD, WIDTH), lambda i: (i, 0))
STATS = pl.BlockSpec((16, PAIRS * HD), lambda i: (0, i))


def call(kernel, name, operands, in_specs, outs, out_specs, scratch, limit, grid=(), cost=1, alias=None):
    results = pl.pallas_call(
        kernel,
        name=name,
        grid=grid,
        out_shape=[jax.ShapeDtypeStruct(shape, dtype) for shape, dtype in outs],
        in_specs=in_specs,
        out_specs=out_specs,
        scratch_shapes=[
            one if not isinstance(one, tuple) else pltpu.VMEM(*one) for one in scratch
        ],
        compiler_params=pltpu.CompilerParams(vmem_limit_bytes=limit * MIB),
        input_output_aliases=alias or {},
        cost_estimate=pl.CostEstimate(
            flops=int(cost * FLOPS), bytes_accessed=0, transcendentals=0
        ),
    )(*operands)
    return list(results)


FLOPS = 1.15e9
GRID = (8 // PAIRS,)
SHARD = ((256, WIDTH), BF16)
WHOLE = ((ROWS, WIDTH), BF16)
PROBS = ((8, HEADS, 512, HD), BF16)
SLOPE = ((8, HEADS, 512, HD), F32)


def pack_call(queries, grads, cond, kv_list, cover_lists):
    return call(
        pack_kernel,
        "pack",
        [queries, grads, cond, kv_list, cover_lists],
        [VMEM] * 5,
        [((592, WIDTH), BF16), ((BLK + 16, WIDTH), BF16)],
        [VMEM] * 2,
        [((16, WIDTH), F32)],
        4,
    )


def stack_call(upper, lower, after):
    return call(
        stack_kernel,
        "stack",
        [upper, lower, after],
        [VMEM] * 2 + [ANY],
        [((512, WIDTH), BF16)],
        [VMEM],
        [],
        2,
    )[0]


def token_call(info, tokens):
    return call(
        token_kernel,
        "tokens",
        [info, tokens],
        [SMEM, HBM],
        [((128, WIDTH), BF16)] * 4,
        [VMEM] * 4,
        [((BLK, 16 * CHUNK), BF16), ((BLK, 16 * PADDED), BF16), pltpu.SemaphoreType.DMA],
        4,
    )


def join_call(parts, tokens):
    return call(
        join_kernel,
        "join",
        parts + tokens,
        [VMEM] * 8,
        [((384, WIDTH), BF16)] * 4 + [((32, HD), jnp.int32)],
        [VMEM] * 5,
        [],
        4,
    )


def tie_kernel(*refs):
    pass


def tied(arrays, after):
    count = len(arrays)
    return call(
        tie_kernel,
        "tie",
        arrays + after,
        [ANY] * count + [VMEM] * len(after),
        [(one.shape, one.dtype) for one in arrays],
        [ANY] * count,
        [],
        4,
        (),
        0.1,
        {n: n for n in range(count)},
    )


def sum_call(parts, after):
    return call(
        sum_kernel,
        "sum",
        parts + after,
        [VMEM] * (4 + len(after)),
        [(parts[0].shape, BF16)],
        [VMEM],
        [],
        4,
    )[0]


def split_call(clip, parts, after):
    return call(
        split_kernel,
        "split",
        [clip] + parts + after,
        [SMEM] + [VMEM] * (4 + len(after)),
        [((96, WIDTH), F32), ((96, WIDTH), BF16)],
        [VMEM] * 2,
        [((CHUNK, WIDTH), F32)],
        4,
    )


def slope_call(info, lists, qg, kv):
    return call(
        slope_kernel,
        "slopes",
        [info, lists] + qg + kv,
        [SMEM] * 2 + [VMEM] * 8,
        [SLOPE, WHOLE],
        [TILES, LINES],
        [WHOLE],
        12,
        GRID,
        4,
    )


def scores_call(info, lists, qg, kv, conds, slope):
    return call(
        score_kernel,
        "scores",
        [info, lists] + qg + kv + conds + [slope],
        [SMEM] * 2 + [VMEM] * 12 + [TILES],
        [WHOLE, ((16, ROWS), F32), PROBS, ((2, 256, WIDTH), BF16)],
        [LINES, STATS, TILES, HBM],
        [WHOLE] * 2 + [pltpu.SemaphoreType.DMA((8,))],
        14,
        GRID,
        5,
    )


def turn_call(kv, after):
    return call(
        turn_kernel,
        "turn",
        kv + after,
        [VMEM] * 5,
        [((16, WIDTH, HD), BF16)] * 2,
        [VMEM] * 2,
        [],
        4,
        (),
        1.2,
    )


def query_call(info, lists, stats, probs, slope, low, high):
    return call(
        query_kernel,
        "query_grads",
        [info, lists] + stats + [probs, slope, low, high],
        [SMEM] * 2 + [VMEM] * 4 + [TILES] * 2 + [VMEM] * 2,
        [SHARD] * 4 + [((512, WIDTH), BF16)] * 2 + [PROBS] * 2,
        [VMEM] * 6 + [TILES] * 2,
        [((8, ROWS), F32)] * 2 + [((ROWS, WIDTH), F32), WHOLE],
        14,
        GRID,
        4.5,
    )


def key_call(info, lists, probs, score, qeff, grads):
    return call(
        key_kernel,
        "key_grads",
        [info, lists, probs, score, qeff, grads],
        [SMEM] * 2 + [TILES] * 2 + [LINES] * 2,
        [WHOLE] * 2 + [((8, HD), F32)],
        [VMEM] * 3,
        [((256, WIDTH), F32)] * 8,
        12,
        GRID,
        5,
    )


def weight_call(info, cond, tokens):
    return call(
        weight_kernel,
        "weights",
        [info, cond, tokens],
        [SMEM, VMEM, HBM],
        [((CHUNK, WIDTH), BF16)] * 4,
        [VMEM] * 4,
        [
            ((2 * CHUNK, WIDTH), F32),
            ((2, 256, 2 * CHUNK), BF16),
            pltpu.SemaphoreType.DMA,
        ],
        8,
        (),
        1,
    )


def body(queries, keys, values, grad_out, kv_list, cover_lists, cond_tokens, cond_weight):
    ctx = lax.axis_index("ctx")
    core = lax.axis_index("head") % 2
    info = lax.dynamic_slice(jnp.asarray(INFO), (core, ctx, 0), (1, 1, 64)).reshape(64)
    cond = jnp.dot(cond_tokens[0], cond_weight, preferred_element_type=F32).astype(BF16)
    kv = stack_call(keys[0], values[0], keys[0])
    qg, row = pack_call(queries[0], grad_out[0], cond, kv_list, cover_lists.T)
    qg1, qg3, row2 = send(qg, "u", 1), send(qg, "u", 3), send(row, "u", 2)
    kv3, kv1 = send(kv, "v", 3), send(kv, "v", 1)
    qg1, kv3 = tied([qg1, kv3], [row2, qg3, kv1])
    out = join_call([qg, qg1, qg3, row2], token_call(info, cond_tokens[0]))
    conds, lists = scattered(out[0:4], "v"), out[4]
    qg = [qg, qg1, qg3, send(qg1, "u", 3)]
    kv = [kv, kv1, kv3, send(kv3, "v", 1)]
    slope, grads = slope_call(info, lists, qg, kv)
    qeff, stat, probs, tokens = scores_call(info, lists, qg, kv, conds, slope)
    stats = gathered(stat, "u")
    low, high = turn_call(kv, [stat])
    out = query_call(info, lists, stats, probs, slope, low, high)
    cg, dq, probs, score = out[0:4], out[4:6], out[6], out[7]
    cg = scattered(cg, "u")
    dkv = key_call(info, lists, probs, score, qeff, grads)
    cg = gathered(sum_call(cg, [dkv[2]]), "v")
    cg = sum_call(cg, [])
    away, = tied([dkv[1]], [cg])
    dkv, on = halved(dkv[0], away, "v", 1, 3)
    dq, dq_on = halved(dq[0], dq[1], "u", 3, 1)
    weight = scattered(weight_call(info, cg, tokens), "u")
    mine, other = split_call(lax.axis_index("dp").reshape(1), weight, [on, dq_on])
    grad_cond_weight = mine + lax.ppermute(other, "dp", [(0, 1), (1, 0)]).astype(F32)
    grad_query = summed(dq).astype(BF16)[None]
    grad_key = summed([part[:256] for part in dkv]).astype(BF16)[None]
    grad_value = summed([part[256:] for part in dkv]).astype(BF16)[None]
    return (grad_query, grad_key, grad_value, grad_cond_weight)


def solution(mesh):
    return jax.shard_map(
        body,
        mesh=mesh,
        in_specs=(
            P("dp", "ctx", "head"),
            P("dp", "ctx", "head"),
            P("dp", "ctx", "head"),
            P("dp", "ctx", "head"),
            P("ctx", None),
            P("ctx", None),
            P("dp", "ctx", None),
            P(None, "head"),
        ),
        out_specs=(
            P("dp", "ctx", "head"),
            P("dp", "ctx", "head"),
            P("dp", "ctx", "head"),
            P(("ctx", "dp"), "head"),
        ),
        check_vma=False,
    )
```

```python
import math

import jax
import jax.numpy as jnp
import numpy as np
from jax import lax
from jax.experimental import pallas as pl
from jax.experimental.pallas import tpu as pltpu
from jax.sharding import PartitionSpec as P

HD = 128
BLK = 64
PER = 2
HEADS = 3
WIDTH = HEADS * HD
SIDE = 4
ROWS = 1024
SCALE = 1.0 / math.sqrt(HD)
LOG2E = 1.4426950408889634
SCALE2 = SCALE * LOG2E
MASKS = (0, 1, 3, 2)
SLOT_OF = {0: 0, 1: 1, 3: 2, 2: 3}
BF16 = jnp.bfloat16
F32 = jnp.float32
MIB = 1 << 20
CHUNK = 192
PADDED = 256
PAIRS = 2


def roles(ctx, core):
    z, x = divmod(ctx, SIDE)
    return (x, z) if core == 0 else (z, x)


def ctx_of(u, v, core):
    return v * SIDE + u if core == 0 else u * SIDE + v


def info_table():
    table = np.zeros((2, SIDE * SIDE, 64), np.int32)
    for core in range(2):
        for ctx in range(SIDE * SIDE):
            u, v = roles(ctx, core)
            row = table[core, ctx]
            for slot, mask in enumerate(MASKS):
                row[slot] = ctx_of(u, v ^ mask, core)
                row[52 + slot] = v ^ mask
            for owner in range(SIDE * SIDE):
                uo, vo = roles(owner, core)
                place = SLOT_OF[vo ^ v] * SIDE + SLOT_OF[uo ^ u]
                row[4 + owner] = place
                row[20 + place] = owner
                row[36 + owner] = SLOT_OF[uo ^ u] * SIDE + vo
    return table


INFO = info_table()


def send(array, role, mask, clip=0):
    pairs = []
    for ctx in range(SIDE * SIDE):
        for head in range(4):
            core = head % 2
            u, v = roles(ctx, core)
            target = ctx_of(u ^ mask, v, core) if role == "u" else ctx_of(u, v ^ mask, core)
            for dp in range(2):
                source = (ctx * 4 + head) * 2 + dp
                pairs.append((source, (target * 4 + head) * 2 + (dp ^ clip)))
    return lax.ppermute(array, ("ctx", "head", "dp"), pairs)


def gathered(array, role):
    return [array] + [send(array, role, mask) for mask in MASKS[1:]]


def scattered(parts, role):
    return parts[:1] + [send(parts[slot], role, MASKS[slot]) for slot in range(1, SIDE)]


def halved(near, away, role, first, second):
    come = send(away, role, first)

    half = near.shape[0] // 2
    on = (near[half:].astype(F32) + come[half:].astype(F32)).astype(BF16)
    return [near[:half], come[:half], send(on, role, second)], on


def summed(parts):
    total = parts[0].astype(F32)
    for part in parts[1:]:
        total = total + part.astype(F32)
    return total


def aligned(ref, mask):
    parts = []
    for mine in MASKS:
        slot = SLOT_OF[mine ^ mask]
        parts.append(ref[:, slot * 256 : (slot + 1) * 256])
    return jnp.concatenate(parts, axis=1)


def nt(a, b):
    return lax.dot_general(a, b, (((1,), (1,)), ((), ())), preferred_element_type=F32)


def nn(a, b):
    return lax.dot_general(a, b, (((1,), (0,)), ((), ())), preferred_element_type=F32)


def tn(a, b):
    return lax.dot_general(a, b, (((0,), (0,)), ((), ())), preferred_element_type=F32)


def picks(info, lists, pair, slot):
    shard = info[slot]
    starts = []
    for block in range(2):
        row = (pair // 2) * 8 + (pair % 2) * 2 + block
        local = [lists[row, shard * PER + j] - shard * SIDE for j in range(PER)]
        starts.append([pl.multiple_of(at * BLK, BLK) for at in local])
    return starts


def columns(head):
    return slice(head * HD, (head + 1) * HD)


def taken(source, starts, head):
    ref, first = source
    at = columns(head)
    rows = [
        jnp.concatenate(
            [ref[pl.ds(first + starts[block][j], BLK), at] for block in range(2)], axis=1
        )
        for j in range(PER)
    ]
    return jnp.concatenate(rows, axis=0)


def diagonal(pair_rows):
    nothing = jnp.zeros((BLK, HD), pair_rows.dtype)
    return jnp.concatenate(
        [
            jnp.concatenate([pair_rows[:BLK], nothing], axis=1),
            jnp.concatenate([nothing, pair_rows[BLK:]], axis=1),
        ],
        axis=0,
    )


def all_taken(sources, starts, head):
    return jnp.concatenate(
        [taken(sources[slot], starts[slot], head) for slot in range(SIDE)], axis=0
    )


def spread(acc, starts, head, part):
    at = columns(head)
    for slot in range(SIDE):
        for j in range(PER):
            for block in range(2):
                row = slot * HD + j * BLK
                piece = part[row : row + BLK, block * HD : (block + 1) * HD]
                acc[slot][pl.ds(starts[slot][block][j], BLK), at] += piece


def covers(lists, block):
    return [lists[(block // 4) * 8 + 4 + j, block % 4] for j in range(2)]


def cover_places(info, lists, block):
    return [info[4 + owner] for owner in covers(lists, block)]


def pack_kernel(queries, grads, cond, kv_list, cover_lists, out, row, lists):
    lists[...] = jnp.zeros_like(lists)
    lists[0:4, 0:32] = kv_list[...].astype(F32)
    lists[4:6, 0:4] = cover_lists[...].astype(F32)
    row[0:BLK, :] = cond[...]
    row[BLK : BLK + 16, :] = lists[...].astype(BF16)
    out[0:256, :] = queries[...]
    out[256:512, :] = grads[...]
    out[512:592, :] = row[...]


def stack_kernel(upper, lower, _, out):
    half = upper.shape[0]
    out[0:half, :] = upper[...]
    out[half:, :] = lower[...]


def token_kernel(info, tokens, *refs):
    out, padded = refs[0:4], refs[4]
    for n in range(16):
        padded[:, n * PADDED : n * PADDED + CHUNK] = tokens[:, n * CHUNK : (n + 1) * CHUNK]
    for sv in range(SIDE):
        for su in range(SIDE):
            start = pl.multiple_of(info[20 + sv * SIDE + su] * PADDED, PADDED)
            columns_here = padded[:, pl.ds(start, PADDED)]
            row = (su // 2) * BLK
            at = (su % 2) * CHUNK
            out[sv][row : row + BLK, at : at + CHUNK] = columns_here[:, 0:CHUNK]


def join_kernel(*refs):
    parts, tokens, out, lists = refs[0:4], refs[4:8], refs[8:12], refs[12]
    for slot in range(SIDE):
        first = parts[slot].shape[0] - BLK - 16
        rows = parts[slot][first + BLK : first + BLK + 16, 0:HD].astype(F32)
        lists[slot * 8 : (slot + 1) * 8, :] = rows[0:8, :].astype(jnp.int32)
        for other in range(SIDE):
            out[other][slot * BLK : (slot + 1) * BLK, :] = parts[slot][first : first + BLK, :]
        out[slot][256:384, :] = tokens[slot][...]


def sum_kernel(*refs):
    out, flag = refs[-2:]
    total = refs[0][...].astype(F32)
    for part in refs[1:4]:
        total = total + part[...].astype(F32)
    out[...] = total.astype(BF16)
    flag[...] = jnp.zeros_like(flag)


def split_kernel(clip, *refs):
    mine, other, total = refs[-3:]
    total[...] = refs[0][...].astype(F32)
    for part in refs[1:4]:
        total[...] += part[...].astype(F32)
    mine[...] = total[pl.ds(pl.multiple_of(clip[0] * 96, 96), 96), :]
    other[...] = total[pl.ds(pl.multiple_of(96 - clip[0] * 96, 96), 96), :].astype(BF16)


def slope_kernel(info, lists, *refs):
    qg, kv, slope_out, grad_out = refs[0:4], refs[4:8], refs[8], refs[9]
    grads = refs[10]
    step = pl.program_id(0)
    values = [(ref, 256) for ref in kv]

    @pl.when(step == 0)
    def _():
        for slot in range(SIDE):
            grads[slot * 256 : (slot + 1) * 256, :] = qg[slot][256:512, :]

    for n in range(PAIRS):
        pair = step * PAIRS + n
        rows = pl.ds(pl.multiple_of(pair * HD, HD), HD)
        grad = grads[rows, :]
        grad_out[rows, :] = grad
        starts = [picks(info, lists, pair, slot) for slot in range(SIDE)]
        for head in range(HEADS):
            slope_out[pair, head] = nt(
                all_taken(values, starts, head), diagonal(grad[:, columns(head)])
            )


def score_kernel(info, lists, *refs):
    qg, kv, conds, slope = refs[0:4], refs[4:8], refs[8:12], refs[12]
    qeff, stat, probs_out, tokens = refs[13:17]
    queries, cond = refs[17:]
    step = pl.program_id(0)
    keys = [(ref, 0) for ref in kv]

    @pl.when(step == 0)
    def _():
        for slot in range(SIDE):
            for half in range(2):
                first = 256 + half * BLK
                tokens[half, slot * BLK : (slot + 1) * BLK, :] = conds[slot][first : first + BLK, :]
        for slot in range(SIDE):
            at = slice(slot * 256, (slot + 1) * 256)
            queries[at, :] = qg[slot][0:256, :]
            cond[at, :] = conds[slot][0:256, :]

    for n in range(PAIRS):
        pair = step * PAIRS + n
        rows = pl.ds(pl.multiple_of(pair * HD, HD), HD)
        here = slice(n * HD, (n + 1) * HD)
        lifted = []
        for block in range(2):
            places = cover_places(info, lists, 2 * pair + block)
            parts = [
                cond[pl.ds(pl.multiple_of(at * BLK, BLK), BLK), :].astype(F32) for at in places
            ]
            lifted.append(parts[0] + parts[1])
        query = (queries[rows, :].astype(F32) + jnp.concatenate(lifted, axis=0)).astype(BF16)
        qeff[rows, :] = query
        starts = [picks(info, lists, pair, slot) for slot in range(SIDE)]
        tops, totals, weighted = [], [], []
        for head in range(HEADS):
            scores = nt(all_taken(keys, starts, head), diagonal(query[:, columns(head)]))
            top = jnp.max(scores, axis=0, keepdims=True)
            probs = jnp.exp2((scores - top) * SCALE2)
            tops.append(top)
            totals.append(jnp.sum(probs, axis=0, keepdims=True))
            weighted.append(jnp.sum(probs * slope[pair, head], axis=0, keepdims=True))
            probs_out[pair, head] = probs.astype(BF16)
        nothing = [jnp.zeros((16 - 3 * HEADS, HD), F32)]
        stat[:, rows] = jnp.concatenate(tops + totals + weighted + nothing, axis=0)


def turn_kernel(*refs):
    kv, low, high = refs[0:4], refs[5], refs[6]
    left = lax.broadcasted_iota(jnp.int32, (HD, HD), 1) < BLK

    def turn(head, carry):
        at = pl.ds(pl.multiple_of(head * HD, HD), HD)
        for slot in range(SIDE):
            for half in range(2):
                tile = kv[slot][half * HD : (half + 1) * HD, at].astype(F32).T
                rolled = pltpu.roll(tile, BLK, 1)
                block = slot * SIDE + 2 * half
                low[block, at, :] = jnp.where(left, tile, 0.0).astype(BF16)
                high[block, at, :] = jnp.where(left, 0.0, rolled).astype(BF16)
                low[block + 1, at, :] = jnp.where(left, rolled, 0.0).astype(BF16)
                high[block + 1, at, :] = jnp.where(left, 0.0, tile).astype(BF16)
        return carry

    lax.fori_loop(0, HEADS, turn, 0)


def query_kernel(info, lists, *refs):
    stats, probs_in, slope_in = refs[0:4], refs[4], refs[5]
    low, high = refs[6], refs[7]
    cg, dq, probs_out, score_out = refs[8:12], refs[12:14], refs[14], refs[15]
    factors, deltas, cond, qbuf = refs[16:]
    step = pl.program_id(0)

    @pl.when(step == 0)
    def _():
        stat = [stats[0][...]] + [aligned(stats[slot], MASKS[slot]) for slot in range(1, SIDE)]
        tops = [s[0:HEADS] for s in stat]
        top = jnp.maximum(jnp.maximum(tops[0], tops[1]), jnp.maximum(tops[2], tops[3]))
        total = jnp.zeros_like(top)
        weighted = jnp.zeros_like(top)
        for s, t in zip(stat, tops):
            share = jnp.exp2((t - top) * SCALE2)
            total = total + s[HEADS : 2 * HEADS] * share
            weighted = weighted + s[2 * HEADS : 3 * HEADS] * share
        factors[0:HEADS, :] = jnp.exp2((tops[0] - top) * SCALE2) / total
        deltas[0:HEADS, :] = weighted / total
        cond[...] = jnp.zeros_like(cond)

    left = lax.broadcasted_iota(jnp.int32, (HD, HD), 1) < BLK
    for n in range(PAIRS):
        pair = step * PAIRS + n
        rows = pl.ds(pl.multiple_of(pair * HD, HD), HD)
        starts = [picks(info, lists, pair, slot) for slot in range(SIDE)]
        parts = []
        for head in range(HEADS):
            at = columns(head)
            factor, delta = factors[head : head + 1, rows], deltas[head : head + 1, rows]
            probs = probs_in[pair, head].astype(F32) * factor
            score = (probs * (slope_in[pair, head] - delta) * SCALE).astype(BF16)
            probs_out[pair, head] = probs.astype(BF16)
            score_out[pair, head] = score
            keys = []
            for block in range(2):
                across = []
                for slot in range(SIDE):
                    one = [slot * SIDE + (starts[slot][block][j] >> 6) for j in range(PER)]
                    across.append(low[one[0], at, :] + high[one[1], at, :])
                keys.append(jnp.concatenate(across, axis=1))
            turned = nn(jnp.concatenate(keys, axis=0), score)
            parts.append(jnp.where(left, turned[:HD], turned[HD:]).T)
        query_part = jnp.concatenate(parts, axis=1)
        qbuf[rows, :] = query_part.astype(BF16)
        for block in range(2):
            for owner in covers(lists, 2 * pair + block):
                to = info[36 + owner]
                cond[pl.ds(pl.multiple_of(to * BLK, BLK), BLK), :] += query_part[
                    block * BLK : (block + 1) * BLK
                ]

    @pl.when(step == 8 // PAIRS - 1)
    def _():
        for slot in range(SIDE):
            at = slice(slot * 256, (slot + 1) * 256)
            cg[slot][...] = cond[at, :].astype(BF16)
            dq[slot // 2][(slot % 2) * 256 : (slot % 2 + 1) * 256, :] = qbuf[at, :]


def key_kernel(info, lists, probs_in, score_in, qeff, grads, *refs):
    dkv, flag, dk, dv = refs[0:2], refs[2], refs[3:7], refs[7:11]
    step = pl.program_id(0)

    @pl.when(step == 0)
    def _():
        flag[...] = jnp.zeros_like(flag)
        for one in dk + dv:
            one[...] = jnp.zeros_like(one)

    for n in range(PAIRS):
        pair = step * PAIRS + n
        rows = pl.ds(pl.multiple_of(pair * HD, HD), HD)
        starts = [picks(info, lists, pair, slot) for slot in range(SIDE)]
        for head in range(HEADS):
            at = columns(head)
            spread(dk, starts, head, nn(score_in[pair, head], diagonal(qeff[rows, at])))
            spread(dv, starts, head, nn(probs_in[pair, head], diagonal(grads[rows, at])))

    @pl.when(step == 8 // PAIRS - 1)
    def _():
        for slot in range(SIDE):
            half = (slot // 2) * 512
            dkv[slot % 2][half : half + 256, :] = dk[slot][...].astype(BF16)
            dkv[slot % 2][half + 256 : half + 512, :] = dv[slot][...].astype(BF16)


def weight_kernel(info, *refs):
    cond, stacked, out, whole = refs[0], refs[1], refs[2:6], refs[6]
    rows = []
    for slot in range(SIDE):
        rows.append(cond[pl.ds(pl.multiple_of(info[52 + slot] * BLK, BLK), BLK), :])
    half_sums = jnp.concatenate(rows, axis=0)
    for half in range(2):
        whole[...] = tn(stacked[half], half_sums)
        for n in range(2):
            out[2 * half + n][...] = whole[n * CHUNK : (n + 1) * CHUNK, :].astype(BF16)


VMEM = pl.BlockSpec(memory_space=pltpu.VMEM)
SMEM = pl.BlockSpec(memory_space=pltpu.SMEM)
ANY = pl.BlockSpec(memory_space=pl.ANY)
TILES = LINES = STATS = VMEM


def call(kernel, name, operands, in_specs, outs, out_specs, scratch, limit, grid=(), cost=1, alias=None):
    results = pl.pallas_call(
        kernel,
        name=name,
        grid=grid,
        out_shape=[jax.ShapeDtypeStruct(shape, dtype) for shape, dtype in outs],
        in_specs=in_specs,
        out_specs=out_specs,
        scratch_shapes=[
            one if not isinstance(one, tuple) else pltpu.VMEM(*one) for one in scratch
        ],
        compiler_params=pltpu.CompilerParams(vmem_limit_bytes=limit * MIB),
        input_output_aliases=alias or {},
        cost_estimate=pl.CostEstimate(
            flops=int(cost * FLOPS), bytes_accessed=0, transcendentals=0
        ),
    )(*operands)
    return list(results)


FLOPS = 1.15e9
GRID = (8 // PAIRS,)
SHARD = ((256, WIDTH), BF16)
WHOLE = ((ROWS, WIDTH), BF16)
PROBS = ((8, HEADS, 512, HD), BF16)
SLOPE = ((8, HEADS, 512, HD), F32)


def pack_call(queries, grads, cond, kv_list, cover_lists):
    return call(
        pack_kernel,
        "pack",
        [queries, grads, cond, kv_list, cover_lists],
        [VMEM] * 5,
        [((592, WIDTH), BF16), ((BLK + 16, WIDTH), BF16)],
        [VMEM] * 2,
        [((16, WIDTH), F32)],
        4,
    )


def stack_call(upper, lower, after):
    return call(
        stack_kernel,
        "stack",
        [upper, lower, after],
        [VMEM] * 2 + [ANY],
        [((512, WIDTH), BF16)],
        [VMEM],
        [],
        2,
    )[0]


def token_call(info, tokens):
    return call(
        token_kernel,
        "tokens",
        [info, tokens],
        [SMEM, VMEM],
        [((128, WIDTH), BF16)] * 4,
        [VMEM] * 4,
        [((BLK, 16 * PADDED), BF16)],
        4,
    )


def join_call(parts, tokens):
    return call(
        join_kernel,
        "join",
        parts + tokens,
        [VMEM] * 8,
        [((384, WIDTH), BF16)] * 4 + [((32, HD), jnp.int32)],
        [VMEM] * 5,
        [],
        4,
    )


def tie_kernel(*refs):
    pass


def tied(arrays, after):
    count = len(arrays)
    return call(
        tie_kernel,
        "tie",
        arrays + after,
        [ANY] * count + [VMEM] * len(after),
        [(one.shape, one.dtype) for one in arrays],
        [ANY] * count,
        [],
        4,
        (),
        0.1,
        {n: n for n in range(count)},
    )


def sum_call(parts, after):
    return call(
        sum_kernel,
        "sum",
        parts + after,
        [VMEM] * (4 + len(after)),
        [(parts[0].shape, BF16), ((8, HD), F32)],
        [VMEM] * 2,
        [],
        4,
    )


def split_call(clip, parts, after):
    return call(
        split_kernel,
        "split",
        [clip] + parts + after,
        [SMEM] + [VMEM] * (4 + len(after)),
        [((96, WIDTH), F32), ((96, WIDTH), BF16)],
        [VMEM] * 2,
        [((CHUNK, WIDTH), F32)],
        4,
        (),
        10,
    )


def slope_call(info, lists, qg, kv):
    return call(
        slope_kernel,
        "slopes",
        [info, lists] + qg + kv,
        [SMEM] * 2 + [VMEM] * 8,
        [SLOPE, WHOLE],
        [TILES, LINES],
        [WHOLE],
        12,
        GRID,
        4,
    )


def scores_call(info, lists, qg, kv, conds, slope):
    return call(
        score_kernel,
        "scores",
        [info, lists] + qg + kv + conds + [slope],
        [SMEM] * 2 + [VMEM] * 12 + [TILES],
        [WHOLE, ((16, ROWS), F32), PROBS, ((2, 256, WIDTH), BF16)],
        [LINES, STATS, TILES, VMEM],
        [WHOLE] * 2,
        14,
        GRID,
        5,
    )


def turn_call(kv, after):
    return call(
        turn_kernel,
        "turn",
        kv + after,
        [VMEM] * 5,
        [((16, WIDTH, HD), BF16)] * 2,
        [VMEM] * 2,
        [],
        4,
        (),
        1.2,
    )


def query_call(info, lists, stats, probs, slope, low, high):
    return call(
        query_kernel,
        "query_grads",
        [info, lists] + stats + [probs, slope, low, high],
        [SMEM] * 2 + [VMEM] * 4 + [TILES] * 2 + [VMEM] * 2,
        [SHARD] * 4 + [((512, WIDTH), BF16)] * 2 + [PROBS] * 2,
        [VMEM] * 6 + [TILES] * 2,
        [((8, ROWS), F32)] * 2 + [((ROWS, WIDTH), F32), WHOLE],
        14,
        GRID,
        4.5,
    )


def key_call(info, lists, probs, score, qeff, grads):
    return call(
        key_kernel,
        "key_grads",
        [info, lists, probs, score, qeff, grads],
        [SMEM] * 2 + [TILES] * 2 + [LINES] * 2,
        [WHOLE] * 2 + [((8, HD), F32)],
        [VMEM] * 3,
        [((256, WIDTH), F32)] * 8,
        12,
        GRID,
        5,
    )


def weight_call(info, cond, tokens):
    return call(
        weight_kernel,
        "weights",
        [info, cond, tokens],
        [SMEM] + [VMEM] * 2,
        [((CHUNK, WIDTH), BF16)] * 4,
        [VMEM] * 4,
        [((2 * CHUNK, WIDTH), F32)],
        8,
        (),
        1,
    )


def body(queries, keys, values, grad_out, kv_list, cover_lists, cond_tokens, cond_weight):
    ctx = lax.axis_index("ctx")
    core = lax.axis_index("head") % 2
    info = lax.dynamic_slice(jnp.asarray(INFO), (core, ctx, 0), (1, 1, 64)).reshape(64)
    cond = jnp.dot(cond_tokens[0], cond_weight, preferred_element_type=F32).astype(BF16)
    kv = stack_call(keys[0], values[0], keys[0])
    qg, row = pack_call(queries[0], grad_out[0], cond, kv_list, cover_lists.T)
    qg1, qg3, row2 = send(qg, "u", 1), send(qg, "u", 3), send(row, "u", 2)
    kv3, kv1 = send(kv, "v", 3), send(kv, "v", 1)
    tokens = token_call(info, cond_tokens[0])
    qg1, kv3 = tied([qg1, kv3], [row2, qg3, kv1])
    out = join_call([qg, qg1, qg3, row2], tokens)
    conds, lists = scattered(out[0:4], "v"), out[4]
    qg = [qg, qg1, qg3, send(qg1, "u", 3)]
    kv = [kv, kv1, kv3, send(kv3, "v", 1)]
    slope, grads = slope_call(info, lists, qg, kv)
    qeff, stat, probs, tokens = scores_call(info, lists, qg, kv, conds, slope)
    stats = gathered(stat, "u")
    low, high = turn_call(kv, [stat])
    out = query_call(info, lists, stats, probs, slope, low, high)
    cg, dq, probs, score = out[0:4], out[4:6], out[6], out[7]
    cg = scattered(cg, "u")
    dkv = key_call(info, lists, probs, score, qeff, grads)
    cg, flag = sum_call(cg, [dkv[2]])
    cg = sum_call(gathered(cg, "v"), [])[0]
    (away,) = tied([dkv[1]], [flag])
    dkv, on = halved(dkv[0], away, "v", 1, 3)
    dq, dq_on = halved(dq[0], dq[1], "u", 3, 1)
    weight = scattered(weight_call(info, cg, tokens), "u")
    mine, other = split_call(lax.axis_index("dp").reshape(1), weight, [on])
    grad_cond_weight = mine + lax.ppermute(other, "dp", [(0, 1), (1, 0)]).astype(F32)
    grad_query = summed(dq).astype(BF16)[None]
    grad_key = summed([part[:256] for part in dkv]).astype(BF16)[None]
    grad_value = summed([part[256:] for part in dkv]).astype(BF16)[None]
    return (grad_query, grad_key, grad_value, grad_cond_weight)


def solution(mesh):
    return jax.shard_map(
        body,
        mesh=mesh,
        in_specs=(
            P("dp", "ctx", "head"),
            P("dp", "ctx", "head"),
            P("dp", "ctx", "head"),
            P("dp", "ctx", "head"),
            P("ctx", None),
            P("ctx", None),
            P("dp", "ctx", None),
            P(None, "head"),
        ),
        out_specs=(
            P("dp", "ctx", "head"),
            P("dp", "ctx", "head"),
            P("dp", "ctx", "head"),
            P(("ctx", "dp"), "head"),
        ),
        check_vma=False,
    )
```

```python
import math

import jax
import jax.numpy as jnp
import numpy as np
from jax import lax
from jax.experimental import pallas as pl
from jax.experimental.pallas import tpu as pltpu
from jax.sharding import PartitionSpec as P

HD = 128
BLK = 64
PER = 2
HEADS = 3
WIDTH = HEADS * HD
SIDE = 4
ROWS = 1024
SCALE = 1.0 / math.sqrt(HD)
LOG2E = 1.4426950408889634
SCALE2 = SCALE * LOG2E
MASKS = (0, 1, 3, 2)
SLOT_OF = {0: 0, 1: 1, 3: 2, 2: 3}
BF16 = jnp.bfloat16
F32 = jnp.float32
MIB = 1 << 20
CHUNK = 192
PADDED = 256
PAIRS = 2


def roles(ctx, core):
    z, x = divmod(ctx, SIDE)
    return (x, z) if core == 0 else (z, x)


def ctx_of(u, v, core):
    return v * SIDE + u if core == 0 else u * SIDE + v


def info_table():
    table = np.zeros((2, SIDE * SIDE, 64), np.int32)
    for core in range(2):
        for ctx in range(SIDE * SIDE):
            u, v = roles(ctx, core)
            row = table[core, ctx]
            for slot, mask in enumerate(MASKS):
                row[slot] = ctx_of(u, v ^ mask, core)
                row[52 + slot] = v ^ mask
            for owner in range(SIDE * SIDE):
                uo, vo = roles(owner, core)
                place = SLOT_OF[vo ^ v] * SIDE + SLOT_OF[uo ^ u]
                row[4 + owner] = place
                row[20 + place] = owner
                row[36 + owner] = SLOT_OF[uo ^ u] * SIDE + vo
    return table


INFO = info_table()


def send(array, role, mask, clip=0):
    pairs = []
    for ctx in range(SIDE * SIDE):
        for head in range(4):
            core = head % 2
            u, v = roles(ctx, core)
            target = ctx_of(u ^ mask, v, core) if role == "u" else ctx_of(u, v ^ mask, core)
            for dp in range(2):
                source = (ctx * 4 + head) * 2 + dp
                pairs.append((source, (target * 4 + head) * 2 + (dp ^ clip)))
    return lax.ppermute(array, ("ctx", "head", "dp"), pairs)


def gathered(array, role):
    return [array] + [send(array, role, mask) for mask in MASKS[1:]]


def scattered(parts, role):
    return parts[:1] + [send(parts[slot], role, MASKS[slot]) for slot in range(1, SIDE)]


def halved(near, away, role, first, second):
    come = send(away, role, first)

    half = near.shape[0] // 2
    on = (near[half:].astype(F32) + come[half:].astype(F32)).astype(BF16)
    return [near[:half], come[:half], send(on, role, second)], on


def summed(parts):
    total = parts[0].astype(F32)
    for part in parts[1:]:
        total = total + part.astype(F32)
    return total


def aligned(ref, mask):
    parts = []
    for mine in MASKS:
        slot = SLOT_OF[mine ^ mask]
        parts.append(ref[:, slot * 256 : (slot + 1) * 256])
    return jnp.concatenate(parts, axis=1)


def nt(a, b):
    return lax.dot_general(a, b, (((1,), (1,)), ((), ())), preferred_element_type=F32)


def nn(a, b):
    return lax.dot_general(a, b, (((1,), (0,)), ((), ())), preferred_element_type=F32)


def tn(a, b):
    return lax.dot_general(a, b, (((0,), (0,)), ((), ())), preferred_element_type=F32)


def picks(info, lists, pair, slot):
    shard = info[slot]
    starts = []
    for block in range(2):
        row = (pair // 2) * 8 + (pair % 2) * 2 + block
        local = [lists[row, shard * PER + j] - shard * SIDE for j in range(PER)]
        starts.append([pl.multiple_of(at * BLK, BLK) for at in local])
    return starts


def columns(head):
    return slice(head * HD, (head + 1) * HD)


def taken(source, starts, head):
    ref, first = source
    at = columns(head)
    rows = [
        jnp.concatenate(
            [ref[pl.ds(first + starts[block][j], BLK), at] for block in range(2)], axis=1
        )
        for j in range(PER)
    ]
    return jnp.concatenate(rows, axis=0)


def diagonal(pair_rows):
    nothing = jnp.zeros((BLK, HD), pair_rows.dtype)
    return jnp.concatenate(
        [
            jnp.concatenate([pair_rows[:BLK], nothing], axis=1),
            jnp.concatenate([nothing, pair_rows[BLK:]], axis=1),
        ],
        axis=0,
    )


def all_taken(sources, starts, head):
    return jnp.concatenate(
        [taken(sources[slot], starts[slot], head) for slot in range(SIDE)], axis=0
    )


def spread(acc, starts, head, part):
    at = columns(head)
    for slot in range(SIDE):
        for j in range(PER):
            for block in range(2):
                row = slot * HD + j * BLK
                piece = part[row : row + BLK, block * HD : (block + 1) * HD]
                acc[slot][pl.ds(starts[slot][block][j], BLK), at] += piece


def covers(lists, block):
    return [lists[(block // 4) * 8 + 4 + j, block % 4] for j in range(2)]


def cover_places(info, lists, block):
    return [info[4 + owner] for owner in covers(lists, block)]


def pack_kernel(queries, grads, cond, kv_list, cover_lists, out, row, lists):
    lists[...] = jnp.zeros_like(lists)
    lists[0:4, 0:32] = kv_list[...].astype(F32)
    lists[4:6, 0:4] = cover_lists[...].astype(F32)
    row[0:BLK, :] = cond[...]
    row[BLK : BLK + 16, :] = lists[...].astype(BF16)
    out[0:256, :] = queries[...]
    out[256:512, :] = grads[...]
    out[512:592, :] = row[...]


def stack_kernel(upper, lower, _, out):
    half = upper.shape[0]
    out[0:half, :] = upper[...]
    out[half:, :] = lower[...]


def token_kernel(info, tokens, *refs):
    out, padded = refs[0:4], refs[4]
    for n in range(16):
        padded[:, n * PADDED : n * PADDED + CHUNK] = tokens[:, n * CHUNK : (n + 1) * CHUNK]
    for sv in range(SIDE):
        for su in range(SIDE):
            start = pl.multiple_of(info[20 + sv * SIDE + su] * PADDED, PADDED)
            columns_here = padded[:, pl.ds(start, PADDED)]
            row = (su // 2) * BLK
            at = (su % 2) * CHUNK
            out[sv][row : row + BLK, at : at + CHUNK] = columns_here[:, 0:CHUNK]


def join_kernel(*refs):
    parts, tokens, out, lists = refs[0:4], refs[4:8], refs[8:12], refs[12]
    for slot in range(SIDE):
        first = parts[slot].shape[0] - BLK - 16
        rows = parts[slot][first + BLK : first + BLK + 16, 0:HD].astype(F32)
        lists[slot * 8 : (slot + 1) * 8, :] = rows[0:8, :].astype(jnp.int32)
        for other in range(SIDE):
            out[other][slot * BLK : (slot + 1) * BLK, :] = parts[slot][first : first + BLK, :]
        out[slot][256:384, :] = tokens[slot][...]


def sum_kernel(*refs):
    out, flag = refs[-2:]
    total = refs[0][...].astype(F32)
    for part in refs[1:4]:
        total = total + part[...].astype(F32)
    out[...] = total.astype(BF16)
    flag[...] = jnp.zeros_like(flag)


def split_kernel(clip, *refs):
    mine, other, total = refs[-3:]
    total[...] = refs[0][...].astype(F32)
    for part in refs[1:4]:
        total[...] += part[...].astype(F32)
    mine[...] = total[pl.ds(pl.multiple_of(clip[0] * 96, 96), 96), :]
    other[...] = total[pl.ds(pl.multiple_of(96 - clip[0] * 96, 96), 96), :].astype(BF16)


def slope_kernel(info, lists, *refs):
    qg, kv, slope_out, grad_out = refs[0:4], refs[4:8], refs[8], refs[9]
    grads = refs[10]
    step = pl.program_id(0)
    values = [(ref, 256) for ref in kv]

    @pl.when(step == 0)
    def _():
        for slot in range(SIDE):
            grads[slot * 256 : (slot + 1) * 256, :] = qg[slot][256:512, :]

    for n in range(PAIRS):
        pair = step * PAIRS + n
        rows = pl.ds(pl.multiple_of(pair * HD, HD), HD)
        grad = grads[rows, :]
        grad_out[rows, :] = grad
        starts = [picks(info, lists, pair, slot) for slot in range(SIDE)]
        for head in range(HEADS):
            slope_out[pair, head] = nt(
                all_taken(values, starts, head), diagonal(grad[:, columns(head)])
            )


def score_kernel(info, lists, *refs):
    qg, kv, conds, slope = refs[0:4], refs[4:8], refs[8:12], refs[12]
    qeff, stat, probs_out, tokens = refs[13:17]
    queries, cond = refs[17:]
    step = pl.program_id(0)
    keys = [(ref, 0) for ref in kv]

    @pl.when(step == 0)
    def _():
        for slot in range(SIDE):
            for half in range(2):
                first = 256 + half * BLK
                tokens[half, slot * BLK : (slot + 1) * BLK, :] = conds[slot][first : first + BLK, :]
        for slot in range(SIDE):
            at = slice(slot * 256, (slot + 1) * 256)
            queries[at, :] = qg[slot][0:256, :]
            cond[at, :] = conds[slot][0:256, :]

    for n in range(PAIRS):
        pair = step * PAIRS + n
        rows = pl.ds(pl.multiple_of(pair * HD, HD), HD)
        here = slice(n * HD, (n + 1) * HD)
        lifted = []
        for block in range(2):
            places = cover_places(info, lists, 2 * pair + block)
            parts = [
                cond[pl.ds(pl.multiple_of(at * BLK, BLK), BLK), :].astype(F32) for at in places
            ]
            lifted.append(parts[0] + parts[1])
        query = (queries[rows, :].astype(F32) + jnp.concatenate(lifted, axis=0)).astype(BF16)
        qeff[rows, :] = query
        starts = [picks(info, lists, pair, slot) for slot in range(SIDE)]
        tops, totals, weighted = [], [], []
        for head in range(HEADS):
            scores = nt(all_taken(keys, starts, head), diagonal(query[:, columns(head)]))
            top = jnp.max(scores, axis=0, keepdims=True)
            probs = jnp.exp2((scores - top) * SCALE2)
            tops.append(top)
            totals.append(jnp.sum(probs, axis=0, keepdims=True))
            weighted.append(jnp.sum(probs * slope[pair, head], axis=0, keepdims=True))
            probs_out[pair, head] = probs.astype(BF16)
        nothing = [jnp.zeros((16 - 3 * HEADS, HD), F32)]
        stat[:, rows] = jnp.concatenate(tops + totals + weighted + nothing, axis=0)


def turn_kernel(*refs):
    kv, low, high = refs[0:4], refs[5], refs[6]
    left = lax.broadcasted_iota(jnp.int32, (HD, HD), 1) < BLK

    def turn(head, carry):
        at = pl.ds(pl.multiple_of(head * HD, HD), HD)
        for slot in range(SIDE):
            for half in range(2):
                tile = kv[slot][half * HD : (half + 1) * HD, at].astype(F32).T
                rolled = pltpu.roll(tile, BLK, 1)
                block = slot * SIDE + 2 * half
                low[block, at, :] = jnp.where(left, tile, 0.0).astype(BF16)
                high[block, at, :] = jnp.where(left, 0.0, rolled).astype(BF16)
                low[block + 1, at, :] = jnp.where(left, rolled, 0.0).astype(BF16)
                high[block + 1, at, :] = jnp.where(left, 0.0, tile).astype(BF16)
        return carry

    lax.fori_loop(0, HEADS, turn, 0)


def query_kernel(info, lists, *refs):
    stats, probs_in, slope_in = refs[0:4], refs[4], refs[5]
    low, high = refs[6], refs[7]
    cg, dq, probs_out, score_out = refs[8:12], refs[12:14], refs[14], refs[15]
    factors, deltas, cond, qbuf = refs[16:]
    step = pl.program_id(0)

    @pl.when(step == 0)
    def _():
        stat = [stats[0][...]] + [aligned(stats[slot], MASKS[slot]) for slot in range(1, SIDE)]
        tops = [s[0:HEADS] for s in stat]
        top = jnp.maximum(jnp.maximum(tops[0], tops[1]), jnp.maximum(tops[2], tops[3]))
        total = jnp.zeros_like(top)
        weighted = jnp.zeros_like(top)
        for s, t in zip(stat, tops):
            share = jnp.exp2((t - top) * SCALE2)
            total = total + s[HEADS : 2 * HEADS] * share
            weighted = weighted + s[2 * HEADS : 3 * HEADS] * share
        factors[0:HEADS, :] = jnp.exp2((tops[0] - top) * SCALE2) / total
        deltas[0:HEADS, :] = weighted / total
        cond[...] = jnp.zeros_like(cond)

    left = lax.broadcasted_iota(jnp.int32, (HD, HD), 1) < BLK
    for n in range(PAIRS):
        pair = step * PAIRS + n
        rows = pl.ds(pl.multiple_of(pair * HD, HD), HD)
        starts = [picks(info, lists, pair, slot) for slot in range(SIDE)]
        parts = []
        for head in range(HEADS):
            at = columns(head)
            factor, delta = factors[head : head + 1, rows], deltas[head : head + 1, rows]
            probs = probs_in[pair, head].astype(F32) * factor
            score = (probs * (slope_in[pair, head] - delta) * SCALE).astype(BF16)
            probs_out[pair, head] = probs.astype(BF16)
            score_out[pair, head] = score
            keys = []
            for block in range(2):
                across = []
                for slot in range(SIDE):
                    one = [slot * SIDE + (starts[slot][block][j] >> 6) for j in range(PER)]
                    across.append(low[one[0], at, :] + high[one[1], at, :])
                keys.append(jnp.concatenate(across, axis=1))
            turned = nn(jnp.concatenate(keys, axis=0), score)
            parts.append(jnp.where(left, turned[:HD], turned[HD:]).T)
        query_part = jnp.concatenate(parts, axis=1)
        qbuf[rows, :] = query_part.astype(BF16)
        for block in range(2):
            for owner in covers(lists, 2 * pair + block):
                to = info[36 + owner]
                cond[pl.ds(pl.multiple_of(to * BLK, BLK), BLK), :] += query_part[
                    block * BLK : (block + 1) * BLK
                ]

    @pl.when(step == 8 // PAIRS - 1)
    def _():
        for slot in range(SIDE):
            at = slice(slot * 256, (slot + 1) * 256)
            cg[slot][...] = cond[at, :].astype(BF16)
            dq[slot // 2][(slot % 2) * 256 : (slot % 2 + 1) * 256, :] = qbuf[at, :]


def key_kernel(info, lists, probs_in, score_in, qeff, grads, *refs):
    dkv, flag, dk, dv = refs[0:2], refs[2], refs[3:7], refs[7:11]
    step = pl.program_id(0)

    @pl.when(step == 0)
    def _():
        flag[...] = jnp.zeros_like(flag)
        for one in dk + dv:
            one[...] = jnp.zeros_like(one)

    for n in range(PAIRS):
        pair = step * PAIRS + n
        rows = pl.ds(pl.multiple_of(pair * HD, HD), HD)
        starts = [picks(info, lists, pair, slot) for slot in range(SIDE)]
        for head in range(HEADS):
            at = columns(head)
            spread(dk, starts, head, nn(score_in[pair, head], diagonal(qeff[rows, at])))
            spread(dv, starts, head, nn(probs_in[pair, head], diagonal(grads[rows, at])))

    @pl.when(step == 8 // PAIRS - 1)
    def _():
        for slot in range(SIDE):
            half = (slot // 2) * 512
            dkv[slot % 2][half : half + 256, :] = dk[slot][...].astype(BF16)
            dkv[slot % 2][half + 256 : half + 512, :] = dv[slot][...].astype(BF16)


def weight_kernel(info, *refs):
    cond, stacked, out, whole = refs[0], refs[1], refs[2:6], refs[6]
    rows = []
    for slot in range(SIDE):
        rows.append(cond[pl.ds(pl.multiple_of(info[52 + slot] * BLK, BLK), BLK), :])
    half_sums = jnp.concatenate(rows, axis=0)
    for half in range(2):
        whole[...] = tn(stacked[half], half_sums)
        for n in range(2):
            out[2 * half + n][...] = whole[n * CHUNK : (n + 1) * CHUNK, :].astype(BF16)


VMEM = pl.BlockSpec(memory_space=pltpu.VMEM)
SMEM = pl.BlockSpec(memory_space=pltpu.SMEM)
ANY = pl.BlockSpec(memory_space=pl.ANY)
TILES = LINES = STATS = VMEM


def call(kernel, name, operands, in_specs, outs, out_specs, scratch, limit, grid=(), cost=1, alias=None):
    results = pl.pallas_call(
        kernel,
        name=name,
        grid=grid,
        out_shape=[jax.ShapeDtypeStruct(shape, dtype) for shape, dtype in outs],
        in_specs=in_specs,
        out_specs=out_specs,
        scratch_shapes=[
            one if not isinstance(one, tuple) else pltpu.VMEM(*one) for one in scratch
        ],
        compiler_params=pltpu.CompilerParams(vmem_limit_bytes=limit * MIB),
        input_output_aliases=alias or {},
        cost_estimate=pl.CostEstimate(
            flops=int(cost * FLOPS), bytes_accessed=0, transcendentals=0
        ),
    )(*operands)
    return list(results)


FLOPS = 1.15e9
GRID = (8 // PAIRS,)
SHARD = ((256, WIDTH), BF16)
WHOLE = ((ROWS, WIDTH), BF16)
PROBS = ((8, HEADS, 512, HD), BF16)
SLOPE = ((8, HEADS, 512, HD), F32)


def pack_call(queries, grads, cond, kv_list, cover_lists):
    return call(
        pack_kernel,
        "pack",
        [queries, grads, cond, kv_list, cover_lists],
        [VMEM] * 5,
        [((592, WIDTH), BF16), ((BLK + 16, WIDTH), BF16)],
        [VMEM] * 2,
        [((16, WIDTH), F32)],
        4,
    )


def stack_call(upper, lower, after):
    return call(
        stack_kernel,
        "stack",
        [upper, lower, after],
        [VMEM] * 2 + [ANY],
        [((512, WIDTH), BF16)],
        [VMEM],
        [],
        2,
    )[0]


def token_call(info, tokens):
    return call(
        token_kernel,
        "tokens",
        [info, tokens],
        [SMEM, VMEM],
        [((128, WIDTH), BF16)] * 4,
        [VMEM] * 4,
        [((BLK, 16 * PADDED), BF16)],
        4,
    )


def join_call(parts, tokens):
    return call(
        join_kernel,
        "join",
        parts + tokens,
        [VMEM] * 8,
        [((384, WIDTH), BF16)] * 4 + [((32, HD), jnp.int32)],
        [VMEM] * 5,
        [],
        4,
    )


def tie_kernel(*refs):
    pass


def tied(arrays, after):
    count = len(arrays)
    return call(
        tie_kernel,
        "tie",
        arrays + after,
        [ANY] * count + [VMEM] * len(after),
        [(one.shape, one.dtype) for one in arrays],
        [ANY] * count,
        [],
        4,
        (),
        0.1,
        {n: n for n in range(count)},
    )


def sum_call(parts, after):
    return call(
        sum_kernel,
        "sum",
        parts + after,
        [VMEM] * (4 + len(after)),
        [(parts[0].shape, BF16), ((8, HD), F32)],
        [VMEM] * 2,
        [],
        4,
    )


def split_call(clip, parts, after):
    return call(
        split_kernel,
        "split",
        [clip] + parts + after,
        [SMEM] + [VMEM] * (4 + len(after)),
        [((96, WIDTH), F32), ((96, WIDTH), BF16)],
        [VMEM] * 2,
        [((CHUNK, WIDTH), F32)],
        4,
        (),
        10,
    )


def slope_call(info, lists, qg, kv):
    return call(
        slope_kernel,
        "slopes",
        [info, lists] + qg + kv,
        [SMEM] * 2 + [VMEM] * 8,
        [SLOPE, WHOLE],
        [TILES, LINES],
        [WHOLE],
        12,
        GRID,
        4,
    )


def scores_call(info, lists, qg, kv, conds, slope):
    return call(
        score_kernel,
        "scores",
        [info, lists] + qg + kv + conds + [slope],
        [SMEM] * 2 + [VMEM] * 12 + [TILES],
        [WHOLE, ((16, ROWS), F32), PROBS, ((2, 256, WIDTH), BF16)],
        [LINES, STATS, TILES, VMEM],
        [WHOLE] * 2,
        14,
        GRID,
        5,
    )


def turn_call(kv, after):
    return call(
        turn_kernel,
        "turn",
        kv + after,
        [VMEM] * 5,
        [((16, WIDTH, HD), BF16)] * 2,
        [VMEM] * 2,
        [],
        4,
        (),
        1.2,
    )


def query_call(info, lists, stats, probs, slope, low, high):
    return call(
        query_kernel,
        "query_grads",
        [info, lists] + stats + [probs, slope, low, high],
        [SMEM] * 2 + [VMEM] * 4 + [TILES] * 2 + [VMEM] * 2,
        [SHARD] * 4 + [((512, WIDTH), BF16)] * 2 + [PROBS] * 2,
        [VMEM] * 6 + [TILES] * 2,
        [((8, ROWS), F32)] * 2 + [((ROWS, WIDTH), F32), WHOLE],
        14,
        GRID,
        4.5,
    )


def key_call(info, lists, probs, score, qeff, grads):
    return call(
        key_kernel,
        "key_grads",
        [info, lists, probs, score, qeff, grads],
        [SMEM] * 2 + [TILES] * 2 + [LINES] * 2,
        [WHOLE] * 2 + [((8, HD), F32)],
        [VMEM] * 3,
        [((256, WIDTH), F32)] * 8,
        12,
        GRID,
        5,
    )


def weight_call(info, cond, tokens):
    return call(
        weight_kernel,
        "weights",
        [info, cond, tokens],
        [SMEM] + [VMEM] * 2,
        [((CHUNK, WIDTH), BF16)] * 4,
        [VMEM] * 4,
        [((2 * CHUNK, WIDTH), F32)],
        8,
        (),
        1,
    )


def body(queries, keys, values, grad_out, kv_list, cover_lists, cond_tokens, cond_weight):
    ctx = lax.axis_index("ctx")
    core = lax.axis_index("head") % 2
    info = lax.dynamic_slice(jnp.asarray(INFO), (core, ctx, 0), (1, 1, 64)).reshape(64)
    cond = jnp.dot(cond_tokens[0], cond_weight, preferred_element_type=F32).astype(BF16)
    kv = stack_call(keys[0], values[0], keys[0])
    qg, row = pack_call(queries[0], grad_out[0], cond, kv_list, cover_lists.T)
    qg1, qg3, row2 = send(qg, "u", 1), send(qg, "u", 3), send(row, "u", 2)
    kv3, kv1 = send(kv, "v", 3), send(kv, "v", 1)
    tokens = token_call(info, cond_tokens[0])
    qg1, kv3 = tied([qg1, kv3], [row2, qg3, kv1])
    out = join_call([qg, qg1, qg3, row2], tokens)
    conds, lists = scattered(out[0:4], "v"), out[4]
    qg = [qg, qg1, qg3, send(qg1, "u", 3)]
    kv = [kv, kv1, kv3, send(kv3, "v", 1)]
    slope, grads = slope_call(info, lists, qg, kv)
    qeff, stat, probs, tokens = scores_call(info, lists, qg, kv, conds, slope)
    stats = gathered(stat, "u")
    low, high = turn_call(kv, [stat])
    out = query_call(info, lists, stats, probs, slope, low, high)
    cg, dq, probs, score = out[0:4], out[4:6], out[6], out[7]
    cg = scattered(cg, "u")
    dkv = key_call(info, lists, probs, score, qeff, grads)
    cg, flag = sum_call(cg, [dkv[2]])
    cg = summed(gathered(cg, "v")).astype(BF16)
    dkv, on = halved(dkv[0], dkv[1], "v", 1, 3)
    dq, dq_on = halved(dq[0], dq[1], "u", 3, 1)
    weight = scattered(weight_call(info, cg, tokens), "u")
    mine, other = split_call(lax.axis_index("dp").reshape(1), weight, [on])
    grad_cond_weight = mine + lax.ppermute(other, "dp", [(0, 1), (1, 0)]).astype(F32)
    grad_query = summed(dq).astype(BF16)[None]
    grad_key = summed([part[:256] for part in dkv]).astype(BF16)[None]
    grad_value = summed([part[256:] for part in dkv]).astype(BF16)[None]
    return (grad_query, grad_key, grad_value, grad_cond_weight)


def solution(mesh):
    return jax.shard_map(
        body,
        mesh=mesh,
        in_specs=(
            P("dp", "ctx", "head"),
            P("dp", "ctx", "head"),
            P("dp", "ctx", "head"),
            P("dp", "ctx", "head"),
            P("ctx", None),
            P("ctx", None),
            P("dp", "ctx", None),
            P(None, "head"),
        ),
        out_specs=(
            P("dp", "ctx", "head"),
            P("dp", "ctx", "head"),
            P("dp", "ctx", "head"),
            P(("ctx", "dp"), "head"),
        ),
        check_vma=False,
    )
```

```python
import math

import jax
import jax.numpy as jnp
import numpy as np
from jax import lax
from jax.experimental import pallas as pl
from jax.experimental.pallas import tpu as pltpu
from jax.sharding import PartitionSpec as P

HD = 128
BLK = 64
PER = 2
HEADS = 3
WIDTH = HEADS * HD
SIDE = 4
ROWS = 1024
SCALE = 1.0 / math.sqrt(HD)
LOG2E = 1.4426950408889634
SCALE2 = SCALE * LOG2E
MASKS = (0, 1, 3, 2)
SLOT_OF = {0: 0, 1: 1, 3: 2, 2: 3}
BF16 = jnp.bfloat16
F32 = jnp.float32
MIB = 1 << 20
CHUNK = 192
PADDED = 256
PAIRS = 4


def roles(ctx, core):
    z, x = divmod(ctx, SIDE)
    return (x, z) if core == 0 else (z, x)


def ctx_of(u, v, core):
    return v * SIDE + u if core == 0 else u * SIDE + v


def info_table():
    table = np.zeros((2, SIDE * SIDE, 64), np.int32)
    for core in range(2):
        for ctx in range(SIDE * SIDE):
            u, v = roles(ctx, core)
            row = table[core, ctx]
            for slot, mask in enumerate(MASKS):
                row[slot] = ctx_of(u, v ^ mask, core)
                row[52 + slot] = v ^ mask
            for owner in range(SIDE * SIDE):
                uo, vo = roles(owner, core)
                place = SLOT_OF[vo ^ v] * SIDE + SLOT_OF[uo ^ u]
                row[4 + owner] = place
                row[20 + place] = owner
                row[36 + owner] = SLOT_OF[uo ^ u] * SIDE + vo
    return table


INFO = info_table()


def send(array, role, mask, clip=0):
    pairs = []
    for ctx in range(SIDE * SIDE):
        for head in range(4):
            core = head % 2
            u, v = roles(ctx, core)
            target = ctx_of(u ^ mask, v, core) if role == "u" else ctx_of(u, v ^ mask, core)
            for dp in range(2):
                source = (ctx * 4 + head) * 2 + dp
                pairs.append((source, (target * 4 + head) * 2 + (dp ^ clip)))
    return lax.ppermute(array, ("ctx", "head", "dp"), pairs)


def gathered(array, role):
    return [array] + [send(array, role, mask) for mask in MASKS[1:]]


def scattered(parts, role):
    return parts[:1] + [send(parts[slot], role, MASKS[slot]) for slot in range(1, SIDE)]


def halved(near, away, role, first, second):
    come = send(away, role, first)

    half = near.shape[0] // 2
    on = (near[half:].astype(F32) + come[half:].astype(F32)).astype(BF16)
    return [near[:half], come[:half], send(on, role, second)], on


def summed(parts):
    total = parts[0].astype(F32)
    for part in parts[1:]:
        total = total + part.astype(F32)
    return total


def aligned(ref, mask):
    parts = []
    for mine in MASKS:
        slot = SLOT_OF[mine ^ mask]
        parts.append(ref[:, slot * 256 : (slot + 1) * 256])
    return jnp.concatenate(parts, axis=1)


def nt(a, b):
    return lax.dot_general(a, b, (((1,), (1,)), ((), ())), preferred_element_type=F32)


def nn(a, b):
    return lax.dot_general(a, b, (((1,), (0,)), ((), ())), preferred_element_type=F32)


def tn(a, b):
    return lax.dot_general(a, b, (((0,), (0,)), ((), ())), preferred_element_type=F32)


def picks(info, lists, pair, slot):
    shard = info[slot]
    starts = []
    for block in range(2):
        row = (pair // 2) * 8 + (pair % 2) * 2 + block
        local = [lists[row, shard * PER + j] - shard * SIDE for j in range(PER)]
        starts.append([pl.multiple_of(at * BLK, BLK) for at in local])
    return starts


def columns(head):
    return slice(head * HD, (head + 1) * HD)


def taken(source, starts, head):
    ref, first = source
    at = columns(head)
    rows = [
        jnp.concatenate(
            [ref[pl.ds(first + starts[block][j], BLK), at] for block in range(2)], axis=1
        )
        for j in range(PER)
    ]
    return jnp.concatenate(rows, axis=0)


def diagonal(pair_rows):
    nothing = jnp.zeros((BLK, HD), pair_rows.dtype)
    return jnp.concatenate(
        [
            jnp.concatenate([pair_rows[:BLK], nothing], axis=1),
            jnp.concatenate([nothing, pair_rows[BLK:]], axis=1),
        ],
        axis=0,
    )


def all_taken(sources, starts, head):
    return jnp.concatenate(
        [taken(sources[slot], starts[slot], head) for slot in range(SIDE)], axis=0
    )


def spread(acc, starts, head, part):
    at = columns(head)
    for slot in range(SIDE):
        for j in range(PER):
            for block in range(2):
                row = slot * HD + j * BLK
                piece = part[row : row + BLK, block * HD : (block + 1) * HD]
                acc[slot][pl.ds(starts[slot][block][j], BLK), at] += piece


def covers(lists, block):
    return [lists[(block // 4) * 8 + 4 + j, block % 4] for j in range(2)]


def cover_places(info, lists, block):
    return [info[4 + owner] for owner in covers(lists, block)]


def pack_kernel(queries, grads, cond, kv_list, cover_lists, out, row, lists):
    lists[...] = jnp.zeros_like(lists)
    lists[0:4, 0:32] = kv_list[...].astype(F32)
    lists[4:6, 0:4] = cover_lists[...].astype(F32)
    row[0:BLK, :] = cond[...]
    row[BLK : BLK + 16, :] = lists[...].astype(BF16)
    out[0:256, :] = queries[...]
    out[256:512, :] = grads[...]
    out[512:592, :] = row[...]


def stack_kernel(upper, lower, _, out):
    half = upper.shape[0]
    out[0:half, :] = upper[...]
    out[half:, :] = lower[...]


def token_kernel(info, tokens, *refs):
    out, padded = refs[0:4], refs[4]
    for n in range(16):
        padded[:, n * PADDED : n * PADDED + CHUNK] = tokens[:, n * CHUNK : (n + 1) * CHUNK]
    for sv in range(SIDE):
        for su in range(SIDE):
            start = pl.multiple_of(info[20 + sv * SIDE + su] * PADDED, PADDED)
            columns_here = padded[:, pl.ds(start, PADDED)]
            row = (su // 2) * BLK
            at = (su % 2) * CHUNK
            out[sv][row : row + BLK, at : at + CHUNK] = columns_here[:, 0:CHUNK]


def join_kernel(*refs):
    parts, tokens, out, lists = refs[0:4], refs[4:8], refs[8:12], refs[12]
    for slot in range(SIDE):
        first = parts[slot].shape[0] - BLK - 16
        rows = parts[slot][first + BLK : first + BLK + 16, 0:HD].astype(F32)
        lists[slot * 8 : (slot + 1) * 8, :] = rows[0:8, :].astype(jnp.int32)
        for other in range(SIDE):
            out[other][slot * BLK : (slot + 1) * BLK, :] = parts[slot][first : first + BLK, :]
        out[slot][256:384, :] = tokens[slot][...]


def sum_kernel(*refs):
    out, flag = refs[-2:]
    total = refs[0][...].astype(F32)
    for part in refs[1:4]:
        total = total + part[...].astype(F32)
    out[...] = total.astype(BF16)
    flag[...] = jnp.zeros_like(flag)


def split_kernel(clip, *refs):
    mine, other, total = refs[-3:]
    total[...] = refs[0][...].astype(F32)
    for part in refs[1:4]:
        total[...] += part[...].astype(F32)
    mine[...] = total[pl.ds(pl.multiple_of(clip[0] * 96, 96), 96), :]
    other[...] = total[pl.ds(pl.multiple_of(96 - clip[0] * 96, 96), 96), :].astype(BF16)


def slope_kernel(info, lists, *refs):
    qg, kv, slope_out, grad_out = refs[0:4], refs[4:8], refs[8], refs[9]
    grads = refs[10]
    step = pl.program_id(0)
    values = [(ref, 256) for ref in kv]

    @pl.when(step == 0)
    def _():
        for slot in range(SIDE):
            grads[slot * 256 : (slot + 1) * 256, :] = qg[slot][256:512, :]

    for n in range(PAIRS):
        pair = step * PAIRS + n
        rows = pl.ds(pl.multiple_of(pair * HD, HD), HD)
        grad = grads[rows, :]
        grad_out[rows, :] = grad
        starts = [picks(info, lists, pair, slot) for slot in range(SIDE)]
        for head in range(HEADS):
            slope_out[pair, head] = nt(
                all_taken(values, starts, head), diagonal(grad[:, columns(head)])
            )


def score_kernel(info, lists, *refs):
    qg, kv, conds, slope = refs[0:4], refs[4:8], refs[8:12], refs[12]
    qeff, stat, probs_out, tokens = refs[13:17]
    queries, cond = refs[17:]
    step = pl.program_id(0)
    keys = [(ref, 0) for ref in kv]

    @pl.when(step == 0)
    def _():
        for slot in range(SIDE):
            for half in range(2):
                first = 256 + half * BLK
                tokens[half, slot * BLK : (slot + 1) * BLK, :] = conds[slot][first : first + BLK, :]
        for slot in range(SIDE):
            at = slice(slot * 256, (slot + 1) * 256)
            queries[at, :] = qg[slot][0:256, :]
            cond[at, :] = conds[slot][0:256, :]

    for n in range(PAIRS):
        pair = step * PAIRS + n
        rows = pl.ds(pl.multiple_of(pair * HD, HD), HD)
        here = slice(n * HD, (n + 1) * HD)
        lifted = []
        for block in range(2):
            places = cover_places(info, lists, 2 * pair + block)
            parts = [
                cond[pl.ds(pl.multiple_of(at * BLK, BLK), BLK), :].astype(F32) for at in places
            ]
            lifted.append(parts[0] + parts[1])
        query = (queries[rows, :].astype(F32) + jnp.concatenate(lifted, axis=0)).astype(BF16)
        qeff[rows, :] = query
        starts = [picks(info, lists, pair, slot) for slot in range(SIDE)]
        tops, totals, weighted = [], [], []
        for head in range(HEADS):
            scores = nt(all_taken(keys, starts, head), diagonal(query[:, columns(head)]))
            top = jnp.max(scores, axis=0, keepdims=True)
            probs = jnp.exp2((scores - top) * SCALE2)
            tops.append(top)
            totals.append(jnp.sum(probs, axis=0, keepdims=True))
            weighted.append(jnp.sum(probs * slope[pair, head], axis=0, keepdims=True))
            probs_out[pair, head] = probs.astype(BF16)
        nothing = [jnp.zeros((16 - 3 * HEADS, HD), F32)]
        stat[:, rows] = jnp.concatenate(tops + totals + weighted + nothing, axis=0)


def turn_kernel(*refs):
    kv, low, high = refs[0:4], refs[5], refs[6]
    left = lax.broadcasted_iota(jnp.int32, (HD, HD), 1) < BLK

    def turn(head, carry):
        at = pl.ds(pl.multiple_of(head * HD, HD), HD)
        for slot in range(SIDE):
            for half in range(2):
                tile = kv[slot][half * HD : (half + 1) * HD, at].astype(F32).T
                rolled = pltpu.roll(tile, BLK, 1)
                block = slot * SIDE + 2 * half
                low[block, at, :] = jnp.where(left, tile, 0.0).astype(BF16)
                high[block, at, :] = jnp.where(left, 0.0, rolled).astype(BF16)
                low[block + 1, at, :] = jnp.where(left, rolled, 0.0).astype(BF16)
                high[block + 1, at, :] = jnp.where(left, 0.0, tile).astype(BF16)
        return carry

    lax.fori_loop(0, HEADS, turn, 0)


def query_kernel(info, lists, *refs):
    stats, probs_in, slope_in = refs[0:4], refs[4], refs[5]
    low, high = refs[6], refs[7]
    cg, dq, probs_out, score_out = refs[8:12], refs[12:14], refs[14], refs[15]
    factors, deltas, cond, qbuf = refs[16:]
    step = pl.program_id(0)

    @pl.when(step == 0)
    def _():
        stat = [stats[0][...]] + [aligned(stats[slot], MASKS[slot]) for slot in range(1, SIDE)]
        tops = [s[0:HEADS] for s in stat]
        top = jnp.maximum(jnp.maximum(tops[0], tops[1]), jnp.maximum(tops[2], tops[3]))
        total = jnp.zeros_like(top)
        weighted = jnp.zeros_like(top)
        for s, t in zip(stat, tops):
            share = jnp.exp2((t - top) * SCALE2)
            total = total + s[HEADS : 2 * HEADS] * share
            weighted = weighted + s[2 * HEADS : 3 * HEADS] * share
        factors[0:HEADS, :] = jnp.exp2((tops[0] - top) * SCALE2) / total
        deltas[0:HEADS, :] = weighted / total
        cond[...] = jnp.zeros_like(cond)

    left = lax.broadcasted_iota(jnp.int32, (HD, HD), 1) < BLK
    for n in range(PAIRS):
        pair = step * PAIRS + n
        rows = pl.ds(pl.multiple_of(pair * HD, HD), HD)
        starts = [picks(info, lists, pair, slot) for slot in range(SIDE)]
        parts = []
        for head in range(HEADS):
            at = columns(head)
            factor, delta = factors[head : head + 1, rows], deltas[head : head + 1, rows]
            probs = probs_in[pair, head].astype(F32) * factor
            score = (probs * (slope_in[pair, head] - delta) * SCALE).astype(BF16)
            probs_out[pair, head] = probs.astype(BF16)
            score_out[pair, head] = score
            keys = []
            for block in range(2):
                across = []
                for slot in range(SIDE):
                    one = [slot * SIDE + (starts[slot][block][j] >> 6) for j in range(PER)]
                    across.append(low[one[0], at, :] + high[one[1], at, :])
                keys.append(jnp.concatenate(across, axis=1))
            turned = nn(jnp.concatenate(keys, axis=0), score)
            parts.append(jnp.where(left, turned[:HD], turned[HD:]).T)
        query_part = jnp.concatenate(parts, axis=1)
        qbuf[rows, :] = query_part.astype(BF16)
        for block in range(2):
            for owner in covers(lists, 2 * pair + block):
                to = info[36 + owner]
                cond[pl.ds(pl.multiple_of(to * BLK, BLK), BLK), :] += query_part[
                    block * BLK : (block + 1) * BLK
                ]

    @pl.when(step == 8 // PAIRS - 1)
    def _():
        for slot in range(SIDE):
            at = slice(slot * 256, (slot + 1) * 256)
            cg[slot][...] = cond[at, :].astype(BF16)
            dq[slot // 2][(slot % 2) * 256 : (slot % 2 + 1) * 256, :] = qbuf[at, :]


def key_kernel(info, lists, probs_in, score_in, qeff, grads, *refs):
    dkv, flag, dk, dv = refs[0:2], refs[2], refs[3:7], refs[7:11]
    step = pl.program_id(0)

    @pl.when(step == 0)
    def _():
        flag[...] = jnp.zeros_like(flag)
        for one in dk + dv:
            one[...] = jnp.zeros_like(one)

    for n in range(PAIRS):
        pair = step * PAIRS + n
        rows = pl.ds(pl.multiple_of(pair * HD, HD), HD)
        starts = [picks(info, lists, pair, slot) for slot in range(SIDE)]
        for head in range(HEADS):
            at = columns(head)
            spread(dk, starts, head, nn(score_in[pair, head], diagonal(qeff[rows, at])))
            spread(dv, starts, head, nn(probs_in[pair, head], diagonal(grads[rows, at])))

    @pl.when(step == 8 // PAIRS - 1)
    def _():
        for slot in range(SIDE):
            half = (slot // 2) * 512
            dkv[slot % 2][half : half + 256, :] = dk[slot][...].astype(BF16)
            dkv[slot % 2][half + 256 : half + 512, :] = dv[slot][...].astype(BF16)


def weight_kernel(info, *refs):
    cond, stacked, out, whole = refs[0], refs[1], refs[2:6], refs[6]
    rows = []
    for slot in range(SIDE):
        rows.append(cond[pl.ds(pl.multiple_of(info[52 + slot] * BLK, BLK), BLK), :])
    half_sums = jnp.concatenate(rows, axis=0)
    for half in range(2):
        whole[...] = tn(stacked[half], half_sums)
        for n in range(2):
            out[2 * half + n][...] = whole[n * CHUNK : (n + 1) * CHUNK, :].astype(BF16)


VMEM = pl.BlockSpec(memory_space=pltpu.VMEM)
SMEM = pl.BlockSpec(memory_space=pltpu.SMEM)
ANY = pl.BlockSpec(memory_space=pl.ANY)
TILES = LINES = STATS = VMEM


def call(kernel, name, operands, in_specs, outs, out_specs, scratch, limit, grid=(), cost=1, alias=None):
    results = pl.pallas_call(
        kernel,
        name=name,
        grid=grid,
        out_shape=[jax.ShapeDtypeStruct(shape, dtype) for shape, dtype in outs],
        in_specs=in_specs,
        out_specs=out_specs,
        scratch_shapes=[
            one if not isinstance(one, tuple) else pltpu.VMEM(*one) for one in scratch
        ],
        compiler_params=pltpu.CompilerParams(vmem_limit_bytes=limit * MIB),
        input_output_aliases=alias or {},
        cost_estimate=pl.CostEstimate(
            flops=int(cost * FLOPS), bytes_accessed=0, transcendentals=0
        ),
    )(*operands)
    return list(results)


FLOPS = 1.15e9
GRID = (8 // PAIRS,)
SHARD = ((256, WIDTH), BF16)
WHOLE = ((ROWS, WIDTH), BF16)
PROBS = ((8, HEADS, 512, HD), BF16)
SLOPE = ((8, HEADS, 512, HD), F32)


def pack_call(queries, grads, cond, kv_list, cover_lists):
    return call(
        pack_kernel,
        "pack",
        [queries, grads, cond, kv_list, cover_lists],
        [VMEM] * 5,
        [((592, WIDTH), BF16), ((BLK + 16, WIDTH), BF16)],
        [VMEM] * 2,
        [((16, WIDTH), F32)],
        4,
    )


def stack_call(upper, lower, after):
    return call(
        stack_kernel,
        "stack",
        [upper, lower, after],
        [VMEM] * 2 + [ANY],
        [((512, WIDTH), BF16)],
        [VMEM],
        [],
        2,
    )[0]


def token_call(info, tokens):
    return call(
        token_kernel,
        "tokens",
        [info, tokens],
        [SMEM, VMEM],
        [((128, WIDTH), BF16)] * 4,
        [VMEM] * 4,
        [((BLK, 16 * PADDED), BF16)],
        4,
    )


def join_call(parts, tokens):
    return call(
        join_kernel,
        "join",
        parts + tokens,
        [VMEM] * 8,
        [((384, WIDTH), BF16)] * 4 + [((32, HD), jnp.int32)],
        [VMEM] * 5,
        [],
        4,
    )


def tie_kernel(*refs):
    pass


def tied(arrays, after):
    count = len(arrays)
    return call(
        tie_kernel,
        "tie",
        arrays + after,
        [ANY] * count + [VMEM] * len(after),
        [(one.shape, one.dtype) for one in arrays],
        [ANY] * count,
        [],
        4,
        (),
        0.1,
        {n: n for n in range(count)},
    )


def sum_call(parts, after):
    return call(
        sum_kernel,
        "sum",
        parts + after,
        [VMEM] * (4 + len(after)),
        [(parts[0].shape, BF16), ((8, HD), F32)],
        [VMEM] * 2,
        [],
        4,
    )


def split_call(clip, parts, after):
    return call(
        split_kernel,
        "split",
        [clip] + parts + after,
        [SMEM] + [VMEM] * (4 + len(after)),
        [((96, WIDTH), F32), ((96, WIDTH), BF16)],
        [VMEM] * 2,
        [((CHUNK, WIDTH), F32)],
        4,
        (),
        10,
    )


def slope_call(info, lists, qg, kv):
    return call(
        slope_kernel,
        "slopes",
        [info, lists] + qg + kv,
        [SMEM] * 2 + [VMEM] * 8,
        [SLOPE, WHOLE],
        [TILES, LINES],
        [WHOLE],
        12,
        GRID,
        4,
    )


def scores_call(info, lists, qg, kv, conds, slope):
    return call(
        score_kernel,
        "scores",
        [info, lists] + qg + kv + conds + [slope],
        [SMEM] * 2 + [VMEM] * 12 + [TILES],
        [WHOLE, ((16, ROWS), F32), PROBS, ((2, 256, WIDTH), BF16)],
        [LINES, STATS, TILES, VMEM],
        [WHOLE] * 2,
        14,
        GRID,
        5,
    )


def turn_call(kv, after):
    return call(
        turn_kernel,
        "turn",
        kv + after,
        [VMEM] * 5,
        [((16, WIDTH, HD), BF16)] * 2,
        [VMEM] * 2,
        [],
        4,
        (),
        1.2,
    )


def query_call(info, lists, stats, probs, slope, low, high):
    return call(
        query_kernel,
        "query_grads",
        [info, lists] + stats + [probs, slope, low, high],
        [SMEM] * 2 + [VMEM] * 4 + [TILES] * 2 + [VMEM] * 2,
        [SHARD] * 4 + [((512, WIDTH), BF16)] * 2 + [PROBS] * 2,
        [VMEM] * 6 + [TILES] * 2,
        [((8, ROWS), F32)] * 2 + [((ROWS, WIDTH), F32), WHOLE],
        14,
        GRID,
        4.5,
    )


def key_call(info, lists, probs, score, qeff, grads):
    return call(
        key_kernel,
        "key_grads",
        [info, lists, probs, score, qeff, grads],
        [SMEM] * 2 + [TILES] * 2 + [LINES] * 2,
        [WHOLE] * 2 + [((8, HD), F32)],
        [VMEM] * 3,
        [((256, WIDTH), F32)] * 8,
        12,
        GRID,
        5,
    )


def weight_call(info, cond, tokens):
    return call(
        weight_kernel,
        "weights",
        [info, cond, tokens],
        [SMEM] + [VMEM] * 2,
        [((CHUNK, WIDTH), BF16)] * 4,
        [VMEM] * 4,
        [((2 * CHUNK, WIDTH), F32)],
        8,
        (),
        1,
    )


def body(queries, keys, values, grad_out, kv_list, cover_lists, cond_tokens, cond_weight):
    ctx = lax.axis_index("ctx")
    core = lax.axis_index("head") % 2
    info = lax.dynamic_slice(jnp.asarray(INFO), (core, ctx, 0), (1, 1, 64)).reshape(64)
    cond = jnp.dot(cond_tokens[0], cond_weight, preferred_element_type=F32).astype(BF16)
    kv = stack_call(keys[0], values[0], keys[0])
    qg, row = pack_call(queries[0], grad_out[0], cond, kv_list, cover_lists.T)
    qg1, qg3, row2 = send(qg, "u", 1), send(qg, "u", 3), send(row, "u", 2)
    kv3, kv1 = send(kv, "v", 3), send(kv, "v", 1)
    tokens = token_call(info, cond_tokens[0])
    qg1, kv3 = tied([qg1, kv3], [row2, qg3, kv1])
    out = join_call([qg, qg1, qg3, row2], tokens)
    conds, lists = scattered(out[0:4], "v"), out[4]
    qg = [qg, qg1, qg3, send(qg1, "u", 3)]
    kv = [kv, kv1, kv3, send(kv3, "v", 1)]
    slope, grads = slope_call(info, lists, qg, kv)
    qeff, stat, probs, tokens = scores_call(info, lists, qg, kv, conds, slope)
    stats = gathered(stat, "u")
    low, high = turn_call(kv, [stat])
    out = query_call(info, lists, stats, probs, slope, low, high)
    cg, dq, probs, score = out[0:4], out[4:6], out[6], out[7]
    cg = scattered(cg, "u")
    dkv = key_call(info, lists, probs, score, qeff, grads)
    cg, flag = sum_call(cg, [dkv[2]])
    cg = summed(gathered(cg, "v")).astype(BF16)
    dkv, on = halved(dkv[0], dkv[1], "v", 1, 3)
    dq, dq_on = halved(dq[0], dq[1], "u", 3, 1)
    weight = scattered(weight_call(info, cg, tokens), "u")
    mine, other = split_call(lax.axis_index("dp").reshape(1), weight, [on])
    grad_cond_weight = mine + lax.ppermute(other, "dp", [(0, 1), (1, 0)]).astype(F32)
    grad_query = summed(dq).astype(BF16)[None]
    grad_key = summed([part[:256] for part in dkv]).astype(BF16)[None]
    grad_value = summed([part[256:] for part in dkv]).astype(BF16)[None]
    return (grad_query, grad_key, grad_value, grad_cond_weight)


def solution(mesh):
    return jax.shard_map(
        body,
        mesh=mesh,
        in_specs=(
            P("dp", "ctx", "head"),
            P("dp", "ctx", "head"),
            P("dp", "ctx", "head"),
            P("dp", "ctx", "head"),
            P("ctx", None),
            P("ctx", None),
            P("dp", "ctx", None),
            P(None, "head"),
        ),
        out_specs=(
            P("dp", "ctx", "head"),
            P("dp", "ctx", "head"),
            P("dp", "ctx", "head"),
            P(("ctx", "dp"), "head"),
        ),
        check_vma=False,
    )
```

```python
import math

import jax
import jax.numpy as jnp
import numpy as np
from jax import lax
from jax.experimental import pallas as pl
from jax.experimental.pallas import tpu as pltpu
from jax.sharding import PartitionSpec as P

HD = 128
BLK = 64
PER = 2
HEADS = 3
WIDTH = HEADS * HD
SIDE = 4
ROWS = 1024
SCALE = 1.0 / math.sqrt(HD)
LOG2E = 1.4426950408889634
SCALE2 = SCALE * LOG2E
MASKS = (0, 1, 3, 2)
SLOT_OF = {0: 0, 1: 1, 3: 2, 2: 3}
BF16 = jnp.bfloat16
F32 = jnp.float32
MIB = 1 << 20
CHUNK = 192
PADDED = 256
PAIRS = 8


def roles(ctx, core):
    z, x = divmod(ctx, SIDE)
    return (x, z) if core == 0 else (z, x)


def ctx_of(u, v, core):
    return v * SIDE + u if core == 0 else u * SIDE + v


def info_table():
    table = np.zeros((2, SIDE * SIDE, 64), np.int32)
    for core in range(2):
        for ctx in range(SIDE * SIDE):
            u, v = roles(ctx, core)
            row = table[core, ctx]
            for slot, mask in enumerate(MASKS):
                row[slot] = ctx_of(u, v ^ mask, core)
                row[52 + slot] = v ^ mask
            for owner in range(SIDE * SIDE):
                uo, vo = roles(owner, core)
                place = SLOT_OF[vo ^ v] * SIDE + SLOT_OF[uo ^ u]
                row[4 + owner] = place
                row[20 + place] = owner
                row[36 + owner] = SLOT_OF[uo ^ u] * SIDE + vo
    return table


INFO = info_table()


def send(array, role, mask, clip=0):
    pairs = []
    for ctx in range(SIDE * SIDE):
        for head in range(4):
            core = head % 2
            u, v = roles(ctx, core)
            target = ctx_of(u ^ mask, v, core) if role == "u" else ctx_of(u, v ^ mask, core)
            for dp in range(2):
                source = (ctx * 4 + head) * 2 + dp
                pairs.append((source, (target * 4 + head) * 2 + (dp ^ clip)))
    return lax.ppermute(array, ("ctx", "head", "dp"), pairs)


def gathered(array, role):
    return [array] + [send(array, role, mask) for mask in MASKS[1:]]


def scattered(parts, role):
    return parts[:1] + [send(parts[slot], role, MASKS[slot]) for slot in range(1, SIDE)]


def halved(near, away, role, first, second):
    come = send(away, role, first)

    half = near.shape[0] // 2
    on = (near[half:].astype(F32) + come[half:].astype(F32)).astype(BF16)
    return [near[:half], come[:half], send(on, role, second)], on


def summed(parts):
    total = parts[0].astype(F32)
    for part in parts[1:]:
        total = total + part.astype(F32)
    return total


def aligned(ref, mask):
    parts = []
    for mine in MASKS:
        slot = SLOT_OF[mine ^ mask]
        parts.append(ref[:, slot * 256 : (slot + 1) * 256])
    return jnp.concatenate(parts, axis=1)


def nt(a, b):
    return lax.dot_general(a, b, (((1,), (1,)), ((), ())), preferred_element_type=F32)


def nn(a, b):
    return lax.dot_general(a, b, (((1,), (0,)), ((), ())), preferred_element_type=F32)


def tn(a, b):
    return lax.dot_general(a, b, (((0,), (0,)), ((), ())), preferred_element_type=F32)


def picks(info, lists, pair, slot):
    shard = info[slot]
    starts = []
    for block in range(2):
        row = (pair // 2) * 8 + (pair % 2) * 2 + block
        local = [lists[row, shard * PER + j] - shard * SIDE for j in range(PER)]
        starts.append([pl.multiple_of(at * BLK, BLK) for at in local])
    return starts


def columns(head):
    return slice(head * HD, (head + 1) * HD)


def taken(source, starts, head):
    ref, first = source
    at = columns(head)
    rows = [
        jnp.concatenate(
            [ref[pl.ds(first + starts[block][j], BLK), at] for block in range(2)], axis=1
        )
        for j in range(PER)
    ]
    return jnp.concatenate(rows, axis=0)


def diagonal(pair_rows):
    nothing = jnp.zeros((BLK, HD), pair_rows.dtype)
    return jnp.concatenate(
        [
            jnp.concatenate([pair_rows[:BLK], nothing], axis=1),
            jnp.concatenate([nothing, pair_rows[BLK:]], axis=1),
        ],
        axis=0,
    )


def all_taken(sources, starts, head):
    return jnp.concatenate(
        [taken(sources[slot], starts[slot], head) for slot in range(SIDE)], axis=0
    )


def spread(acc, starts, head, part):
    at = columns(head)
    for slot in range(SIDE):
        for j in range(PER):
            for block in range(2):
                row = slot * HD + j * BLK
                piece = part[row : row + BLK, block * HD : (block + 1) * HD]
                acc[slot][pl.ds(starts[slot][block][j], BLK), at] += piece


def covers(lists, block):
    return [lists[(block // 4) * 8 + 4 + j, block % 4] for j in range(2)]


def cover_places(info, lists, block):
    return [info[4 + owner] for owner in covers(lists, block)]


def pack_kernel(queries, grads, cond, kv_list, cover_lists, out, row, lists):
    lists[...] = jnp.zeros_like(lists)
    lists[0:4, 0:32] = kv_list[...].astype(F32)
    lists[4:6, 0:4] = cover_lists[...].astype(F32)
    row[0:BLK, :] = cond[...]
    row[BLK : BLK + 16, :] = lists[...].astype(BF16)
    out[0:256, :] = queries[...]
    out[256:512, :] = grads[...]
    out[512:592, :] = row[...]


def stack_kernel(upper, lower, _, out):
    half = upper.shape[0]
    out[0:half, :] = upper[...]
    out[half:, :] = lower[...]


def token_kernel(info, tokens, *refs):
    out, padded = refs[0:4], refs[4]
    for n in range(16):
        padded[:, n * PADDED : n * PADDED + CHUNK] = tokens[:, n * CHUNK : (n + 1) * CHUNK]
    for sv in range(SIDE):
        for su in range(SIDE):
            start = pl.multiple_of(info[20 + sv * SIDE + su] * PADDED, PADDED)
            columns_here = padded[:, pl.ds(start, PADDED)]
            row = (su // 2) * BLK
            at = (su % 2) * CHUNK
            out[sv][row : row + BLK, at : at + CHUNK] = columns_here[:, 0:CHUNK]


def join_kernel(*refs):
    parts, tokens, out, lists = refs[0:4], refs[4:8], refs[8:12], refs[12]
    for slot in range(SIDE):
        first = parts[slot].shape[0] - BLK - 16
        rows = parts[slot][first + BLK : first + BLK + 16, 0:HD].astype(F32)
        lists[slot * 8 : (slot + 1) * 8, :] = rows[0:8, :].astype(jnp.int32)
        for other in range(SIDE):
            out[other][slot * BLK : (slot + 1) * BLK, :] = parts[slot][first : first + BLK, :]
        out[slot][256:384, :] = tokens[slot][...]


def sum_kernel(*refs):
    out, flag = refs[-2:]
    total = refs[0][...].astype(F32)
    for part in refs[1:4]:
        total = total + part[...].astype(F32)
    out[...] = total.astype(BF16)
    flag[...] = jnp.zeros_like(flag)


def split_kernel(clip, *refs):
    mine, other, total = refs[-3:]
    total[...] = refs[0][...].astype(F32)
    for part in refs[1:4]:
        total[...] += part[...].astype(F32)
    mine[...] = total[pl.ds(pl.multiple_of(clip[0] * 96, 96), 96), :]
    other[...] = total[pl.ds(pl.multiple_of(96 - clip[0] * 96, 96), 96), :].astype(BF16)


def slope_kernel(info, lists, *refs):
    qg, kv, slope_out, grad_out = refs[0:4], refs[4:8], refs[8], refs[9]
    grads = refs[10]
    step = pl.program_id(0)
    values = [(ref, 256) for ref in kv]

    @pl.when(step == 0)
    def _():
        for slot in range(SIDE):
            grads[slot * 256 : (slot + 1) * 256, :] = qg[slot][256:512, :]

    for n in range(PAIRS):
        pair = step * PAIRS + n
        rows = pl.ds(pl.multiple_of(pair * HD, HD), HD)
        grad = grads[rows, :]
        grad_out[rows, :] = grad
        starts = [picks(info, lists, pair, slot) for slot in range(SIDE)]
        for head in range(HEADS):
            slope_out[pair, head] = nt(
                all_taken(values, starts, head), diagonal(grad[:, columns(head)])
            )


def score_kernel(info, lists, *refs):
    qg, kv, conds, slope = refs[0:4], refs[4:8], refs[8:12], refs[12]
    qeff, stat, probs_out, tokens = refs[13:17]
    queries, cond = refs[17:]
    step = pl.program_id(0)
    keys = [(ref, 0) for ref in kv]

    @pl.when(step == 0)
    def _():
        for slot in range(SIDE):
            for half in range(2):
                first = 256 + half * BLK
                tokens[half, slot * BLK : (slot + 1) * BLK, :] = conds[slot][first : first + BLK, :]
        for slot in range(SIDE):
            at = slice(slot * 256, (slot + 1) * 256)
            queries[at, :] = qg[slot][0:256, :]
            cond[at, :] = conds[slot][0:256, :]

    for n in range(PAIRS):
        pair = step * PAIRS + n
        rows = pl.ds(pl.multiple_of(pair * HD, HD), HD)
        here = slice(n * HD, (n + 1) * HD)
        lifted = []
        for block in range(2):
            places = cover_places(info, lists, 2 * pair + block)
            parts = [
                cond[pl.ds(pl.multiple_of(at * BLK, BLK), BLK), :].astype(F32) for at in places
            ]
            lifted.append(parts[0] + parts[1])
        query = (queries[rows, :].astype(F32) + jnp.concatenate(lifted, axis=0)).astype(BF16)
        qeff[rows, :] = query
        starts = [picks(info, lists, pair, slot) for slot in range(SIDE)]
        tops, totals, weighted = [], [], []
        for head in range(HEADS):
            scores = nt(all_taken(keys, starts, head), diagonal(query[:, columns(head)]))
            top = jnp.max(scores, axis=0, keepdims=True)
            probs = jnp.exp2((scores - top) * SCALE2)
            tops.append(top)
            totals.append(jnp.sum(probs, axis=0, keepdims=True))
            weighted.append(jnp.sum(probs * slope[pair, head], axis=0, keepdims=True))
            probs_out[pair, head] = probs.astype(BF16)
        nothing = [jnp.zeros((16 - 3 * HEADS, HD), F32)]
        stat[:, rows] = jnp.concatenate(tops + totals + weighted + nothing, axis=0)


def turn_kernel(*refs):
    kv, low, high = refs[0:4], refs[5], refs[6]
    left = lax.broadcasted_iota(jnp.int32, (HD, HD), 1) < BLK

    def turn(head, carry):
        at = pl.ds(pl.multiple_of(head * HD, HD), HD)
        for slot in range(SIDE):
            for half in range(2):
                tile = kv[slot][half * HD : (half + 1) * HD, at].astype(F32).T
                rolled = pltpu.roll(tile, BLK, 1)
                block = slot * SIDE + 2 * half
                low[block, at, :] = jnp.where(left, tile, 0.0).astype(BF16)
                high[block, at, :] = jnp.where(left, 0.0, rolled).astype(BF16)
                low[block + 1, at, :] = jnp.where(left, rolled, 0.0).astype(BF16)
                high[block + 1, at, :] = jnp.where(left, 0.0, tile).astype(BF16)
        return carry

    lax.fori_loop(0, HEADS, turn, 0)


def query_kernel(info, lists, *refs):
    stats, probs_in, slope_in = refs[0:4], refs[4], refs[5]
    low, high = refs[6], refs[7]
    cg, dq, probs_out, score_out = refs[8:12], refs[12:14], refs[14], refs[15]
    factors, deltas, cond, qbuf = refs[16:]
    step = pl.program_id(0)

    @pl.when(step == 0)
    def _():
        stat = [stats[0][...]] + [aligned(stats[slot], MASKS[slot]) for slot in range(1, SIDE)]
        tops = [s[0:HEADS] for s in stat]
        top = jnp.maximum(jnp.maximum(tops[0], tops[1]), jnp.maximum(tops[2], tops[3]))
        total = jnp.zeros_like(top)
        weighted = jnp.zeros_like(top)
        for s, t in zip(stat, tops):
            share = jnp.exp2((t - top) * SCALE2)
            total = total + s[HEADS : 2 * HEADS] * share
            weighted = weighted + s[2 * HEADS : 3 * HEADS] * share
        factors[0:HEADS, :] = jnp.exp2((tops[0] - top) * SCALE2) / total
        deltas[0:HEADS, :] = weighted / total
        cond[...] = jnp.zeros_like(cond)

    left = lax.broadcasted_iota(jnp.int32, (HD, HD), 1) < BLK
    for n in range(PAIRS):
        pair = step * PAIRS + n
        rows = pl.ds(pl.multiple_of(pair * HD, HD), HD)
        starts = [picks(info, lists, pair, slot) for slot in range(SIDE)]
        parts = []
        for head in range(HEADS):
            at = columns(head)
            factor, delta = factors[head : head + 1, rows], deltas[head : head + 1, rows]
            probs = probs_in[pair, head].astype(F32) * factor
            score = (probs * (slope_in[pair, head] - delta) * SCALE).astype(BF16)
            probs_out[pair, head] = probs.astype(BF16)
            score_out[pair, head] = score
            keys = []
            for block in range(2):
                across = []
                for slot in range(SIDE):
                    one = [slot * SIDE + (starts[slot][block][j] >> 6) for j in range(PER)]
                    across.append(low[one[0], at, :] + high[one[1], at, :])
                keys.append(jnp.concatenate(across, axis=1))
            turned = nn(jnp.concatenate(keys, axis=0), score)
            parts.append(jnp.where(left, turned[:HD], turned[HD:]).T)
        query_part = jnp.concatenate(parts, axis=1)
        qbuf[rows, :] = query_part.astype(BF16)
        for block in range(2):
            for owner in covers(lists, 2 * pair + block):
                to = info[36 + owner]
                cond[pl.ds(pl.multiple_of(to * BLK, BLK), BLK), :] += query_part[
                    block * BLK : (block + 1) * BLK
                ]

    @pl.when(step == 8 // PAIRS - 1)
    def _():
        for slot in range(SIDE):
            at = slice(slot * 256, (slot + 1) * 256)
            cg[slot][...] = cond[at, :].astype(BF16)
            dq[slot // 2][(slot % 2) * 256 : (slot % 2 + 1) * 256, :] = qbuf[at, :]


def key_kernel(info, lists, probs_in, score_in, qeff, grads, *refs):
    dkv, flag, dk, dv = refs[0:2], refs[2], refs[3:7], refs[7:11]
    step = pl.program_id(0)

    @pl.when(step == 0)
    def _():
        flag[...] = jnp.zeros_like(flag)
        for one in dk + dv:
            one[...] = jnp.zeros_like(one)

    for n in range(PAIRS):
        pair = step * PAIRS + n
        rows = pl.ds(pl.multiple_of(pair * HD, HD), HD)
        starts = [picks(info, lists, pair, slot) for slot in range(SIDE)]
        for head in range(HEADS):
            at = columns(head)
            spread(dk, starts, head, nn(score_in[pair, head], diagonal(qeff[rows, at])))
            spread(dv, starts, head, nn(probs_in[pair, head], diagonal(grads[rows, at])))

    @pl.when(step == 8 // PAIRS - 1)
    def _():
        for slot in range(SIDE):
            half = (slot // 2) * 512
            dkv[slot % 2][half : half + 256, :] = dk[slot][...].astype(BF16)
            dkv[slot % 2][half + 256 : half + 512, :] = dv[slot][...].astype(BF16)


def weight_kernel(info, *refs):
    cond, stacked, out, whole = refs[0], refs[1], refs[2:6], refs[6]
    rows = []
    for slot in range(SIDE):
        rows.append(cond[pl.ds(pl.multiple_of(info[52 + slot] * BLK, BLK), BLK), :])
    half_sums = jnp.concatenate(rows, axis=0)
    for half in range(2):
        whole[...] = tn(stacked[half], half_sums)
        for n in range(2):
            out[2 * half + n][...] = whole[n * CHUNK : (n + 1) * CHUNK, :].astype(BF16)


VMEM = pl.BlockSpec(memory_space=pltpu.VMEM)
SMEM = pl.BlockSpec(memory_space=pltpu.SMEM)
ANY = pl.BlockSpec(memory_space=pl.ANY)
TILES = LINES = STATS = VMEM


def call(kernel, name, operands, in_specs, outs, out_specs, scratch, limit, grid=(), cost=1, alias=None):
    results = pl.pallas_call(
        kernel,
        name=name,
        grid=grid,
        out_shape=[jax.ShapeDtypeStruct(shape, dtype) for shape, dtype in outs],
        in_specs=in_specs,
        out_specs=out_specs,
        scratch_shapes=[
            one if not isinstance(one, tuple) else pltpu.VMEM(*one) for one in scratch
        ],
        compiler_params=pltpu.CompilerParams(vmem_limit_bytes=limit * MIB),
        input_output_aliases=alias or {},
        cost_estimate=pl.CostEstimate(
            flops=int(cost * FLOPS), bytes_accessed=0, transcendentals=0
        ),
    )(*operands)
    return list(results)


FLOPS = 1.15e9
GRID = (8 // PAIRS,)
SHARD = ((256, WIDTH), BF16)
WHOLE = ((ROWS, WIDTH), BF16)
PROBS = ((8, HEADS, 512, HD), BF16)
SLOPE = ((8, HEADS, 512, HD), F32)


def pack_call(queries, grads, cond, kv_list, cover_lists):
    return call(
        pack_kernel,
        "pack",
        [queries, grads, cond, kv_list, cover_lists],
        [VMEM] * 5,
        [((592, WIDTH), BF16), ((BLK + 16, WIDTH), BF16)],
        [VMEM] * 2,
        [((16, WIDTH), F32)],
        4,
    )


def stack_call(upper, lower, after):
    return call(
        stack_kernel,
        "stack",
        [upper, lower, after],
        [VMEM] * 2 + [ANY],
        [((512, WIDTH), BF16)],
        [VMEM],
        [],
        2,
    )[0]


def token_call(info, tokens):
    return call(
        token_kernel,
        "tokens",
        [info, tokens],
        [SMEM, VMEM],
        [((128, WIDTH), BF16)] * 4,
        [VMEM] * 4,
        [((BLK, 16 * PADDED), BF16)],
        4,
    )


def join_call(parts, tokens):
    return call(
        join_kernel,
        "join",
        parts + tokens,
        [VMEM] * 8,
        [((384, WIDTH), BF16)] * 4 + [((32, HD), jnp.int32)],
        [VMEM] * 5,
        [],
        4,
    )


def tie_kernel(*refs):
    pass


def tied(arrays, after):
    count = len(arrays)
    return call(
        tie_kernel,
        "tie",
        arrays + after,
        [ANY] * count + [VMEM] * len(after),
        [(one.shape, one.dtype) for one in arrays],
        [ANY] * count,
        [],
        4,
        (),
        0.1,
        {n: n for n in range(count)},
    )


def sum_call(parts, after):
    return call(
        sum_kernel,
        "sum",
        parts + after,
        [VMEM] * (4 + len(after)),
        [(parts[0].shape, BF16), ((8, HD), F32)],
        [VMEM] * 2,
        [],
        4,
    )


def split_call(clip, parts, after):
    return call(
        split_kernel,
        "split",
        [clip] + parts + after,
        [SMEM] + [VMEM] * (4 + len(after)),
        [((96, WIDTH), F32), ((96, WIDTH), BF16)],
        [VMEM] * 2,
        [((CHUNK, WIDTH), F32)],
        4,
        (),
        10,
    )


def slope_call(info, lists, qg, kv):
    return call(
        slope_kernel,
        "slopes",
        [info, lists] + qg + kv,
        [SMEM] * 2 + [VMEM] * 8,
        [SLOPE, WHOLE],
        [TILES, LINES],
        [WHOLE],
        12,
        GRID,
        4,
    )


def scores_call(info, lists, qg, kv, conds, slope):
    return call(
        score_kernel,
        "scores",
        [info, lists] + qg + kv + conds + [slope],
        [SMEM] * 2 + [VMEM] * 12 + [TILES],
        [WHOLE, ((16, ROWS), F32), PROBS, ((2, 256, WIDTH), BF16)],
        [LINES, STATS, TILES, VMEM],
        [WHOLE] * 2,
        14,
        GRID,
        5,
    )


def turn_call(kv, after):
    return call(
        turn_kernel,
        "turn",
        kv + after,
        [VMEM] * 5,
        [((16, WIDTH, HD), BF16)] * 2,
        [VMEM] * 2,
        [],
        4,
        (),
        1.2,
    )


def query_call(info, lists, stats, probs, slope, low, high):
    return call(
        query_kernel,
        "query_grads",
        [info, lists] + stats + [probs, slope, low, high],
        [SMEM] * 2 + [VMEM] * 4 + [TILES] * 2 + [VMEM] * 2,
        [SHARD] * 4 + [((512, WIDTH), BF16)] * 2 + [PROBS] * 2,
        [VMEM] * 6 + [TILES] * 2,
        [((8, ROWS), F32)] * 2 + [((ROWS, WIDTH), F32), WHOLE],
        14,
        GRID,
        4.5,
    )


def key_call(info, lists, probs, score, qeff, grads):
    return call(
        key_kernel,
        "key_grads",
        [info, lists, probs, score, qeff, grads],
        [SMEM] * 2 + [TILES] * 2 + [LINES] * 2,
        [WHOLE] * 2 + [((8, HD), F32)],
        [VMEM] * 3,
        [((256, WIDTH), F32)] * 8,
        12,
        GRID,
        5,
    )


def weight_call(info, cond, tokens):
    return call(
        weight_kernel,
        "weights",
        [info, cond, tokens],
        [SMEM] + [VMEM] * 2,
        [((CHUNK, WIDTH), BF16)] * 4,
        [VMEM] * 4,
        [((2 * CHUNK, WIDTH), F32)],
        8,
        (),
        1,
    )


def body(queries, keys, values, grad_out, kv_list, cover_lists, cond_tokens, cond_weight):
    ctx = lax.axis_index("ctx")
    core = lax.axis_index("head") % 2
    info = lax.dynamic_slice(jnp.asarray(INFO), (core, ctx, 0), (1, 1, 64)).reshape(64)
    cond = jnp.dot(cond_tokens[0], cond_weight, preferred_element_type=F32).astype(BF16)
    kv = stack_call(keys[0], values[0], keys[0])
    qg, row = pack_call(queries[0], grad_out[0], cond, kv_list, cover_lists.T)
    qg1, qg3, row2 = send(qg, "u", 1), send(qg, "u", 3), send(row, "u", 2)
    kv3, kv1 = send(kv, "v", 3), send(kv, "v", 1)
    tokens = token_call(info, cond_tokens[0])
    qg1, kv3 = tied([qg1, kv3], [row2, qg3, kv1])
    out = join_call([qg, qg1, qg3, row2], tokens)
    conds, lists = scattered(out[0:4], "v"), out[4]
    qg = [qg, qg1, qg3, send(qg1, "u", 3)]
    kv = [kv, kv1, kv3, send(kv3, "v", 1)]
    slope, grads = slope_call(info, lists, qg, kv)
    qeff, stat, probs, tokens = scores_call(info, lists, qg, kv, conds, slope)
    stats = gathered(stat, "u")
    low, high = turn_call(kv, [stat])
    out = query_call(info, lists, stats, probs, slope, low, high)
    cg, dq, probs, score = out[0:4], out[4:6], out[6], out[7]
    cg = scattered(cg, "u")
    dkv = key_call(info, lists, probs, score, qeff, grads)
    cg, flag = sum_call(cg, [dkv[2]])
    cg = summed(gathered(cg, "v")).astype(BF16)
    dkv, on = halved(dkv[0], dkv[1], "v", 1, 3)
    dq, dq_on = halved(dq[0], dq[1], "u", 3, 1)
    weight = scattered(weight_call(info, cg, tokens), "u")
    mine, other = split_call(lax.axis_index("dp").reshape(1), weight, [on])
    grad_cond_weight = mine + lax.ppermute(other, "dp", [(0, 1), (1, 0)]).astype(F32)
    grad_query = summed(dq).astype(BF16)[None]
    grad_key = summed([part[:256] for part in dkv]).astype(BF16)[None]
    grad_value = summed([part[256:] for part in dkv]).astype(BF16)[None]
    return (grad_query, grad_key, grad_value, grad_cond_weight)


def solution(mesh):
    return jax.shard_map(
        body,
        mesh=mesh,
        in_specs=(
            P("dp", "ctx", "head"),
            P("dp", "ctx", "head"),
            P("dp", "ctx", "head"),
            P("dp", "ctx", "head"),
            P("ctx", None),
            P("ctx", None),
            P("dp", "ctx", None),
            P(None, "head"),
        ),
        out_specs=(
            P("dp", "ctx", "head"),
            P("dp", "ctx", "head"),
            P("dp", "ctx", "head"),
            P(("ctx", "dp"), "head"),
        ),
        check_vma=False,
    )
```
